128 devices in a mesh: seq: 32 (over y, z, core), head: 4 (over x).
Axes of the slice: x: 4, y: 4, z: 4, core: 2. Of those that a mesh axis runs over, the one named last changes fastest.
Arguments:
- hidden: bfloat16 [8192, 2048], P('seq'), may hold values from -45 to 45, as said below
- w_query: bfloat16 [2048, 2048], P(None, 'head'), may hold values from -0.125 to 0.125
- w_key: bfloat16 [2048, 2048], P(None, 'head'), may hold values from -0.125 to 0.125
- w_value: bfloat16 [2048, 4096], P(None, 'head'), may hold values from -0.125 to 0.125
- w_gate_z: bfloat16 [2048, 4096], P(None, 'head'), may hold values from -0.125 to 0.125
- w_decay: bfloat16 [2048, 32], P(None, 'head'), may hold values from -0.125 to 0.125
- w_beta: bfloat16 [2048, 32], P(None, 'head'), may hold values from -0.125 to 0.125
- conv_query: bfloat16 [4, 2048], P(None, 'head'), may hold values from -3 to 3
- conv_key: bfloat16 [4, 2048], P(None, 'head'), may hold values from -3 to 3
- conv_value: bfloat16 [4, 4096], P(None, 'head'), may hold values from -3 to 3
- decay_log: float32 [32], P('head'), may hold values from -3.6 to -0.69
- decay_bias: float32 [32], P('head'), may hold values from -13 to 0.5
- beta_bias: float32 [32], P('head'), may hold values from -5.5 to 1
- norm_gain: float32 [128], replicated, may hold values from 0.5 to 1.5
- w_out: bfloat16 [4096, 2048], P('head'), may hold values from -0.09375 to 0.09375
- state_in: float32 [32, 128, 128], P('head'), may hold values from -0.6 to 0.6
Outputs:
- mixed: bfloat16 [8192, 2048], P(('seq', 'head'))
The draws below stay inside these ranges and needn't reach their ends.
Inputs may be any that keep to these rules, and one draw needn't show every extreme that they name: `hidden`: activations of order one with a few rows of ten times that size.
All inputs are finite; a program needn't handle non-finite values.
Results may differ from the reference program's by a relative error of at most 0.0062.
Values may be sent and summed in bfloat16 or wider, within the bound.
A program may use at most 128 MiB of HBM per device.

```python
import math
import jax
import jax.numpy as jnp
from jax import lax

D = 2048
HK = 16
HV = 32
DK = 128
DV = 128
KS = 4
TOKENS = 8192


def head_kinds(key, share):
    return jax.random.uniform(jax.random.fold_in(key, 100), (HV,)) < share


def draw_hidden(key, part):
    key = jax.random.fold_in(key, 1)
    key_base = jax.random.fold_in(key, 11)
    key_spots = jax.random.fold_in(key, 13)
    base = jax.random.normal(key_base, (TOKENS, D), jnp.float32)
    base = jnp.clip(base, -4.5, 4.5)
    spots = jax.random.randint(key_spots, (6,), 0, TOKENS)
    marked = jnp.any(jnp.arange(TOKENS)[:, None] == spots[None, :], axis=1)
    factor = jnp.where(marked, 10.0, 1.0).astype(jnp.float32)
    return (base * factor[:, None]).astype(jnp.bfloat16)


def draw_decay_log(key, part):
    fast = head_kinds(key, 0.5)
    key = jax.random.fold_in(key, 2)
    fast_val = jax.random.uniform(jax.random.fold_in(key, 21), (HV,), jnp.float32, math.log(0.03), math.log(0.08))
    slow_val = jax.random.uniform(jax.random.fold_in(key, 22), (HV,), jnp.float32, math.log(0.2), math.log(0.5))
    return jnp.where(fast, fast_val, slow_val)


def draw_decay_bias(key, part):
    fast = head_kinds(key, 0.5)
    key = jax.random.fold_in(key, 3)
    fast_val = jax.random.uniform(jax.random.fold_in(key, 31), (HV,), jnp.float32, -0.5, 0.5)
    slow_val = jax.random.uniform(jax.random.fold_in(key, 32), (HV,), jnp.float32, -13.0, -11.0)
    return jnp.where(fast, fast_val, slow_val)


def draw_beta_bias(key, part):
    fast = head_kinds(key, 0.5)
    key = jax.random.fold_in(key, 4)
    fast_val = jax.random.uniform(jax.random.fold_in(key, 41), (HV,), jnp.float32, -1.0, 1.0)
    slow_val = jax.random.uniform(jax.random.fold_in(key, 42), (HV,), jnp.float32, -5.5, -4.5)
    return jnp.where(fast, fast_val, slow_val)


def block_levels(rng, extent, pieces, smallest, largest):
    factor_of = 1.0
    for position, parts in pieces:
        draws = jax.random.uniform(jax.random.fold_in(jax.random.fold_in(rng, 6), position), (parts,), jnp.float32, smallest / len(pieces), largest / len(pieces))
        factor_of = factor_of * jnp.repeat(jnp.exp(draws), extent[position] // parts).reshape((-1,) + (1,) * (len(extent) - 1 - position))
    return factor_of


def gaussian(own_key, extent, scale, limit, cuts=(), kind=jnp.bfloat16):
    drawn = jax.random.normal(own_key, extent, jnp.float32) * scale
    if len(cuts) > 0:
        drawn = block_levels(own_key, extent, cuts, -0.22, 0.18) * drawn
    return jnp.clip(drawn, min=-limit, max=limit).astype(kind)


def setup_inputs(seed: int = 0) -> dict:
    arg_keys = jax.random.split(jax.random.key(seed), 17)
    return {
        "hidden": draw_hidden(jax.random.fold_in(arg_keys[16], 71), 0),
        "w_query": gaussian(arg_keys[1], (D, HK * DK), D ** -0.5, 0.125, ((1, 4),)),
        "w_key": gaussian(arg_keys[2], (D, HK * DK), D ** -0.5, 0.125, ((1, 4),)),
        "w_value": gaussian(arg_keys[3], (D, HV * DV), D ** -0.5, 0.125, ((1, 4),)),
        "w_gate_z": gaussian(arg_keys[4], (D, HV * DV), D ** -0.5, 0.125, ((1, 4),)),
        "w_decay": gaussian(arg_keys[5], (D, HV), D ** -0.5, 0.125, ((1, 4),)),
        "w_beta": gaussian(arg_keys[6], (D, HV), D ** -0.5, 0.125, ((1, 4),)),
        "conv_query": gaussian(arg_keys[7], (KS, HK * DK), KS ** -0.5, 3.0, ((1, 4),)),
        "conv_key": gaussian(arg_keys[8], (KS, HK * DK), KS ** -0.5, 3.0, ((1, 4),)),
        "conv_value": gaussian(arg_keys[9], (KS, HV * DV), KS ** -0.5, 3.0, ((1, 4),)),
        "decay_log": draw_decay_log(jax.random.fold_in(arg_keys[16], 71), 0),
        "decay_bias": draw_decay_bias(jax.random.fold_in(arg_keys[16], 71), 0),
        "beta_bias": draw_beta_bias(jax.random.fold_in(arg_keys[16], 71), 0),
        "norm_gain": jnp.clip(1.0 + 0.1 * jax.random.normal(arg_keys[13], (DV,), jnp.float32), 0.5, 1.5),
        "w_out": gaussian(arg_keys[14], (HV * DV, D), (HV * DV) ** -0.5, 0.09375, ((0, 4),)),
        "state_in": gaussian(arg_keys[15], (HV, DK, DV), 0.1, 0.6, ((0, 4),), jnp.float32),
    }


def conv_act(raw, taps_weight):
    taps = taps_weight.shape[0]
    rows = raw.shape[0]
    padded = jnp.concatenate([jnp.zeros((taps - 1, raw.shape[1]), jnp.float32), raw.astype(jnp.float32)], 0)
    total = jnp.zeros((rows, raw.shape[1]), jnp.float32)
    for tap in range(taps):
        total = total + taps_weight[tap].astype(jnp.float32) * padded[tap:tap + rows]
    return jax.nn.silu(total)

def unit_rows(values):
    return values * lax.rsqrt(lax.optimization_barrier(jnp.sum(values * values, axis=-1, keepdims=True)) + 1e-06)

def reference(hidden, w_query, w_key, w_value, w_gate_z, w_decay, w_beta, conv_query, conv_key, conv_value, decay_log, decay_bias, beta_bias, norm_gain, w_out, state_in):
    peak_magnitude = lax.Precision.HIGHEST
    query_raw = jnp.dot(hidden, w_query, preferred_element_type=jnp.float32).astype(jnp.bfloat16)
    key_raw = jnp.dot(hidden, w_key, preferred_element_type=jnp.float32).astype(jnp.bfloat16)
    value_raw = jnp.dot(hidden, w_value, preferred_element_type=jnp.float32).astype(jnp.bfloat16)
    query = unit_rows(conv_act(query_raw, conv_query).reshape(TOKENS, HK, DK)) * DK ** (-0.5)
    keys = unit_rows(conv_act(key_raw, conv_key).reshape(TOKENS, HK, DK))
    values = conv_act(value_raw, conv_value).reshape(TOKENS, HV, DV)
    gate_log = -jnp.exp(decay_log) * jax.nn.softplus(jnp.dot(hidden, w_decay, preferred_element_type=jnp.float32) + decay_bias)
    strength = jax.nn.sigmoid(jnp.dot(hidden, w_beta, preferred_element_type=jnp.float32) + beta_bias)
    gate_z = jnp.dot(hidden, w_gate_z, preferred_element_type=jnp.float32).reshape(TOKENS, HV, DV)
    query = jnp.repeat(query, HV // HK, axis=1)
    keys = jnp.repeat(keys, HV // HK, axis=1)

    def advance(running_state, inputs):
        query_at_token, key_at_token, value_t, gate_t, strength_t = inputs
        running_state = jnp.exp(gate_t)[:, None, None] * running_state
        initial_estimate = jnp.einsum('fd,fdl->fl', key_at_token, running_state, precision=peak_magnitude)
        state_update = strength_t[:, None] * (value_t - initial_estimate)
        running_state = running_state + jnp.einsum('pn,pq->pnq', key_at_token, state_update, precision=peak_magnitude)
        layer_output = jnp.einsum('fd,fdl->fl', query_at_token, running_state, precision=peak_magnitude)
        return (running_state, layer_output)
    final_state, core = lax.scan(advance, state_in, (query, keys, values, gate_log, strength))
    scale = lax.rsqrt(lax.optimization_barrier(jnp.mean(core * core, axis=-1, keepdims=True)) + 1e-06)
    normed = (core * scale * norm_gain * jax.nn.silu(gate_z)).astype(jnp.bfloat16).reshape(TOKENS, HV * DV)
    return jnp.dot(normed, w_out, preferred_element_type=jnp.float32).astype(jnp.bfloat16)
```

```python
import jax
import jax.numpy as jnp
from jax import lax
from jax.experimental import pallas as pl
from jax.experimental.pallas import tpu as pltpu
from jax.sharding import PartitionSpec as P

MESH = pl.DeviceIdType.MESH
F32 = jnp.float32
BF16 = jnp.bfloat16
HALO = 16
OWN = 256
ROWS = 512
DM = 2048
CH = 128
NC = ROWS // CH
HEADS = 4
CHIPS = 16
MSG = 208


def dot(a, b):
    return jnp.dot(a, b, preferred_element_type=F32)


def dot_nt(a, b):
    return lax.dot_general(a, b, (((1,), (1,)), ((), ())), preferred_element_type=F32)


def silu(u):
    return u * jax.nn.sigmoid(u)


def kernel(
    hidden, w_query, w_key, w_value, w_gate_z, w_decay, w_beta, conv_query, conv_key, conv_value,
    decay_log, decay_bias, beta_bias, norm_gain, w_out, state_in,
    out,
    hid, wbuf, wdec, wbet, wo, st0, raw, qs, ks, vs, zs, cum, cumt, beta, low, tri, att, uw, ee, sb, ab,
    reach, outloc, send, recv, step_out, entering, nsend, nfull, rs_send, rs_relay, rs_arr, rs_own, rs_hold,
    lsem, wsem, xsem, hsem, msend, mrecv, osend, orecv, nsem, rsend, rrecv,
):
    seq = lax.axis_index("seq")
    xx = lax.axis_index("head")
    chip = seq // 2
    core = seq % 2
    other = 1 - core
    partner = (chip * 2 + other, xx)
    nxt = lax.rem(chip + 1, CHIPS)
    prv = lax.rem(chip + CHIPS - 1, CHIPS)
    right = lax.rem(xx + 1, 4)
    left = lax.rem(xx + 3, 4)
    across = lax.rem(xx + 2, 4)

    def at_x(x):
        return (seq, x)

    def local(src, dst, sem):
        return pltpu.make_async_copy(src, dst, sem)

    def remote(src, dst, s_sem, r_sem, device):
        return pltpu.make_async_remote_copy(
            src_ref=src, dst_ref=dst, send_sem=s_sem, recv_sem=r_sem, device_id=device, device_id_type=MESH
        )

    mine = pl.ds(pl.multiple_of(HALO + core * OWN, 16), OWN)
    theirs = pl.ds(pl.multiple_of(HALO + other * OWN, 16), OWN)
    col256 = pl.ds(pl.multiple_of(core * 256, 256), 256)

    own_copy = local(hidden, hid.at[mine, :], lsem.at[0])
    own_copy.start()
    w_copies = [
        local(w_query.at[:, col256], wbuf.at[0], wsem.at[0]),
        local(w_key.at[:, col256], wbuf.at[1], wsem.at[1]),
    ]
    for i in range(2):
        cols = pl.ds(pl.multiple_of(core * 512 + i * 256, 256), 256)
        w_copies.append(local(w_value.at[:, cols], wbuf.at[2 + i], wsem.at[2 + i]))
    for i in range(2):
        cols = pl.ds(pl.multiple_of(core * 512 + i * 256, 256), 256)
        w_copies.append(local(w_gate_z.at[:, cols], wbuf.at[4 + i], wsem.at[4 + i]))
    dec_copy = local(w_decay, wdec, lsem.at[1])
    bet_copy = local(w_beta, wbet, lsem.at[2])
    for cp in w_copies[:2]:
        cp.start()
    dec_copy.start()
    bet_copy.start()
    for cp in w_copies[2:]:
        cp.start()
    owner_head = core * HEADS + chip // 4
    owner_slot = chip // 2
    st_copy = local(state_in.at[owner_head], st0, lsem.at[3])
    st_copy.start()
    wo_copy = local(w_out, wo, lsem.at[4])
    wo_copy.start()

    barrier = pltpu.get_barrier_semaphore()

    def greet(device):
        pl.semaphore_signal(barrier, inc=1, device_id=device, device_id_type=MESH)

    greet(partner)
    greet((lax.select(core == 1, nxt * 2, prv * 2 + 1), xx))
    greet(at_x(right))
    greet(at_x(left))

    def greet_chip(k, carry):
        greet((lax.rem(chip + k, CHIPS) * 2 + core, xx))
        return carry

    lax.fori_loop(1, CHIPS, greet_chip, 0)
    pl.semaphore_wait(barrier, 19)

    swap = remote(hidden, hid.at[mine, :], xsem.at[0], xsem.at[1], partner)
    swap.start()
    tail = hidden.at[pl.ds(OWN - HALO, HALO), :]
    halo0 = remote(tail, hid.at[pl.ds(0, HALO), :], hsem.at[0], hsem.at[2], (nxt * 2, xx))
    halo1 = remote(tail, hid.at[pl.ds(0, HALO), :], hsem.at[1], hsem.at[2], (nxt * 2 + 1, xx))

    @pl.when(core == 1)
    def _():
        halo0.start()
        halo1.start()

    own_copy.wait()
    swap.wait_recv()
    halo0.wait_recv()

    @pl.when(chip == 0)
    def _():
        hid[pl.ds(0, HALO), :] = jnp.zeros((HALO, DM), BF16)

    taps_of = (
        lambda: conv_query[:, col256].astype(F32),
        lambda: conv_key[:, col256].astype(F32),
        lambda: conv_value[:, pl.ds(pl.multiple_of(core * 512, 256), 256)].astype(F32),
        lambda: conv_value[:, pl.ds(pl.multiple_of(core * 512 + 256, 256), 256)].astype(F32),
    )
    for b in range(4):
        w_copies[b].wait()

        def rows_of(t, carry, b=b):
            r = pl.ds(pl.multiple_of(t * 176, 16), 176)
            raw[b, r, :] = dot(hid[r, :], wbuf[b]).astype(BF16).astype(F32)
            return carry

        lax.fori_loop(0, 3, rows_of, 0)
        taps = taps_of[b]()
        for t in range(NC):
            pre = jnp.zeros((CH, 256), F32)
            for i in range(4):
                pre = pre + taps[i : i + 1, :] * raw[b, pl.ds(HALO - 3 + i + t * CH, CH), :]
            act = silu(pre)
            r = pl.ds(t * CH, CH)
            if b < 2:
                for g in range(2):
                    a = act[:, g * 128 : (g + 1) * 128]
                    n = a * lax.rsqrt(jnp.sum(a * a, axis=-1, keepdims=True) + 1e-6)
                    if b == 0:
                        qs[r, g * 128 : (g + 1) * 128] = (n * 128 ** (-0.5)).astype(BF16)
                    else:
                        ks[r, g * 128 : (g + 1) * 128] = n.astype(BF16)
            else:
                vs[r, (b - 2) * 256 : (b - 1) * 256] = act

    dec_copy.wait()
    bet_copy.wait()
    lane = lax.broadcasted_iota(jnp.int32, (1, HEADS), 1)

    def lanes_of(ref):
        v = jnp.zeros((1, HEADS), F32)
        for h in range(HEADS):
            v = jnp.where(lane == h, ref[core * HEADS + h], v)
        return v

    rate = -jnp.exp(lanes_of(decay_log))
    d_bias = lanes_of(decay_bias)
    b_bias = lanes_of(beta_bias)
    ti = lax.broadcasted_iota(jnp.int32, (CH, CH), 0)
    tj = lax.broadcasted_iota(jnp.int32, (CH, CH), 1)
    incl = ti >= tj
    ones_low = jnp.where(incl, 1.0, 0.0).astype(F32)
    for t in range(NC):
        hrows = hid[pl.ds(HALO + t * CH, CH), :]
        gd = dot(hrows, wdec[...])
        gb = dot(hrows, wbet[...])
        gd = jnp.where(core == 0, gd[:, :HEADS], gd[:, HEADS:])
        gb = jnp.where(core == 0, gb[:, :HEADS], gb[:, HEADS:])
        u = gd + d_bias
        soft = jnp.maximum(u, 0.0) + jnp.log1p(jnp.exp(-jnp.abs(u)))
        glog = jnp.concatenate([rate * soft, jnp.zeros((CH, 128 - HEADS), F32)], 1)
        cm = jnp.dot(ones_low, glog, precision=lax.Precision.HIGHEST, preferred_element_type=F32)
        cum[t] = cm
        cumt[t] = cm.T[:8, :]
        beta[t] = jnp.concatenate([jax.nn.sigmoid(gb + b_bias), jnp.zeros((CH, 128 - HEADS), F32)], 1)

    def systems(c, carry):
        r = pl.ds(pl.multiple_of(c * CH, CH), CH)
        cc_all = cum[c]
        cr_all = cumt[c]
        be_all = beta[c]
        for g in range(2):
            k = ks[r, g * 128 : (g + 1) * 128]
            q = qs[r, g * 128 : (g + 1) * 128]
            both = dot_nt(jnp.concatenate([k, q], 0), k)
            kk, qk = both[:CH], both[CH:]
            for e in range(2):
                h = 2 * g + e
                diff = cc_all[:, h : h + 1] - cr_all[h : h + 1, :]
                ratio = jnp.exp(jnp.where(incl, diff, -1e30))
                lo = jnp.where(ti > tj, be_all[:, h : h + 1] * ratio * kk, 0.0)
                low[c * 2 + g, :, e * 128 : (e + 1) * 128] = lo.astype(BF16)
                att[c * 4 + h] = (ratio * qk).astype(BF16)
                tri[c * 2 + g, :, e * 128 : (e + 1) * 128] = jnp.where(
                    ti == tj, 1.0, jnp.where((ti ^ tj) == 1, -lo, 0.0)
                ).astype(BF16)
        return carry

    lax.fori_loop(0, NC, systems, 0)

    z128 = jnp.zeros((CH, CH), BF16)

    def pair_diag(m):
        return jnp.concatenate(
            [jnp.concatenate([m[:, :128], z128], 1), jnp.concatenate([z128, m[:, 128:]], 1)], 0
        )

    pi = lax.broadcasted_iota(jnp.int32, (CH, 256), 0)
    pj = lax.broadcasted_iota(jnp.int32, (CH, 256), 1) % 128
    pxor = pi ^ pj

    def double(level, size):
        mask = (pxor >= size) & (pxor < 2 * size)
        prods = []
        for p in range(8):
            lm = jnp.where(mask, low[p].astype(F32), 0.0).astype(BF16)
            prods.append(dot(tri[p], pair_diag(lm)).astype(BF16))
        for p in range(8):
            t_old = tri[p]
            y = dot(prods[p], pair_diag(t_old))
            tri[p] = (t_old.astype(F32) - y).astype(BF16)
        return size * 2

    lax.fori_loop(0, 6, double, jnp.int32(2))

    def unit(c, carry):
        r = pl.ds(pl.multiple_of(c * CH, CH), CH)
        cc_all = cum[c]
        cr_all = cumt[c]
        be_all = beta[c]
        for g in range(2):
            k = ks[r, g * 128 : (g + 1) * 128].astype(F32)
            kt = k.T
            for e in range(2):
                h = 2 * g + e
                be = be_all[:, h : h + 1]
                cc = cc_all[:, h : h + 1]
                cr = cr_all[h : h + 1, :]
                tail_w = jnp.exp(cr[:, 127:128] - cr)
                rhs = jnp.concatenate([be * vs[r, h * 128 : (h + 1) * 128], (be * jnp.exp(cc)) * k], 1)
                u = dot(tri[c * 2 + g, :, e * 128 : (e + 1) * 128], rhs.astype(BF16)).astype(BF16)
                uw[c * 4 + h] = u
                ee[c * 4 + h] = dot((kt * tail_w).astype(BF16), u)
        return carry

    lax.fori_loop(0, NC, unit, 0)

    row16 = lax.broadcasted_iota(jnp.int32, (16, 128), 0)
    s_cur, b_cur, a_cur = [], [], []
    for h in range(HEADS):
        e0 = ee[h]
        s_cur.append(e0[:, :128])
        b_cur.append(-e0[:, 128:])
        a_cur.append(jnp.exp(cumt[0, h : h + 1, 127:128]))
        sb[h] = jnp.zeros((128, 256), BF16)
        ab[0, h : h + 1, :] = jnp.ones((1, 128), F32)
    for c in range(1, NC):
        for h in range(HEADS):
            s, bm, a = s_cur[h], b_cur[h], a_cur[h]
            packed = jnp.concatenate([s, bm], 1).astype(BF16)
            sb[c * 4 + h] = packed
            ab[c, h : h + 1, :] = jnp.broadcast_to(a, (1, 128))
            e_c = ee[c * 4 + h]
            m_c = e_c[:, 128:]
            p = dot(m_c.astype(BF16), packed)
            al = jnp.exp(cumt[c, h : h + 1, 127:128])
            s_cur[h] = al * s - p[:, :128] + e_c[:, :128]
            b_cur[h] = al * bm - a * m_c - p[:, 128:]
            a_cur[h] = a * al
    for h in range(HEADS):
        bt = b_cur[h].T.astype(BF16)
        s_t = s_cur[h].T.astype(BF16)
        a_full = jnp.broadcast_to(a_cur[h], (16, 128))
        a_hi = a_full.astype(BF16).astype(F32)
        a_rows = jnp.where(row16 < 8, a_hi, a_full - a_hi).astype(BF16)
        for half in range(2):
            o = 2 * h + half
            send[o, 0:128, :] = bt
            send[o, 128:192, :] = s_t[half * 64 : (half + 1) * 64, :]
            send[o, 192:208, :] = a_rows

    def to_owner(o):
        return remote(send.at[o], recv.at[chip], msend.at[o], mrecv.at[chip], ((2 * o + core) * 2 + core, xx))

    for o in range(8):
        @pl.when(2 * o + core != chip)
        def _(o=o):
            to_owner(o).start()

        @pl.when(2 * o + core == chip)
        def _(o=o):
            recv[chip] = send[o]

    def local_part(c, carry):
        r = pl.ds(pl.multiple_of(c * CH, CH), CH)
        cc_all = cum[c]
        a_all = ab[c]
        for h in range(HEADS):
            g = h // 2
            q = qs[r, g * 128 : (g + 1) * 128].astype(F32)
            o = dot(att[c * 4 + h], uw[c * 4 + h])
            qeff = jnp.exp(cc_all[:, h : h + 1]) * q - o[:, 128:]
            rr = dot(qeff.astype(BF16), sb[c * 4 + h])
            outloc[r, h * 128 : (h + 1) * 128] = o[:, :128] + rr[:, :128]
            reach[r, h * 128 : (h + 1) * 128] = (a_all[h : h + 1, :] * qeff + rr[:, 128:]).astype(BF16)
        return carry

    lax.fori_loop(0, NC, local_part, 0)

    owns = lax.rem(chip, 2) == core
    st_copy.wait()

    def give(i):
        return remote(step_out.at[i], entering.at[owner_slot], osend.at[i], orecv.at[owner_slot], (i * 2 + core, xx))

    @pl.when(owns)
    def _():
        for i in range(CHIPS):
            @pl.when(i != chip)
            def _(i=i):
                remote(send.at[0], recv.at[i], msend.at[0], mrecv.at[i], partner).wait_recv()
        st_t = st0[...].T
        s = jnp.where(lax.rem(owner_slot, 2) == 0, st_t[:64], st_t[64:])
        for i in range(CHIPS):
            sbf = s.astype(BF16)
            step_out[i] = sbf

            @pl.when(i != chip)
            def _(i=i):
                give(i).start()

            if i < CHIPS - 1:
                a = recv[i, 192:208, :].astype(F32)
                s = (a[0:1, :] + a[8:9, :]) * s + dot(sbf, recv[i, 0:128, :]) + recv[i, 128:192, :].astype(F32)
        entering[owner_slot] = step_out[chip]

    for b in range(2):
        w_copies[4 + b].wait()
    gain = jnp.concatenate([norm_gain[...].reshape(1, 128)] * 2, 1)

    def gate_rows(t, carry):
        r = pl.ds(pl.multiple_of(t * CH, CH), CH)
        h_rows = hid[pl.ds(pl.multiple_of(HALO + t * CH, 16), CH), :]
        for b in range(2):
            zs[r, b * 256 : (b + 1) * 256] = silu(dot(h_rows, wbuf[4 + b])) * gain
        return carry

    lax.fori_loop(0, NC, gate_rows, 0)

    for o in range(8):
        @pl.when(2 * o + core != chip)
        def _(o=o):
            remote(step_out.at[0], entering.at[o], osend.at[0], orecv.at[o], partner).wait_recv()

    def finish(base, put):
        for t in range(2):
            r = pl.ds(pl.multiple_of(base + t * CH, CH), CH)
            for h in range(HEADS):
                cols = slice(h * 128, (h + 1) * 128)
                s_t = jnp.concatenate([entering[2 * h], entering[2 * h + 1]], 0)
                o = outloc[r, cols] + dot_nt(reach[r, cols], s_t)
                n = o * lax.rsqrt(jnp.mean(o * o, axis=-1, keepdims=True) + 1e-6) * zs[r, cols]
                put(t, cols, n.astype(BF16))

    def put_send(t, cols, v):
        nsend[t * CH : (t + 1) * CH, cols] = v

    def put_own(t, cols, v):
        nfull[core, t * CH : (t + 1) * CH, cols] = v

    finish(other * OWN, put_send)
    n_swap = remote(nsend, nfull.at[core], nsem.at[0], nsem.at[1], partner)
    n_swap.start()
    finish(core * OWN, put_own)
    wo_copy.wait()
    n_swap.wait_recv()

    def block(x, n0, width):
        r = pl.ds(pl.multiple_of(x * 64, 64), 64)
        cols = slice(n0, n0 + width)
        return dot(nfull[0, r, :], wo[0:512, cols]) + dot(nfull[1, r, :], wo[512:1024, cols])

    def fill(dst, x, n0):
        for j in range(2):
            dst[:, j * 512 : (j + 1) * 512] = block(x, n0 + j * 512, 512).astype(BF16)

    relay_r = remote(rs_send.at[0], rs_relay.at[0], rsend.at[0], rrecv.at[0], at_x(right))
    relay_l = remote(rs_send.at[1], rs_relay.at[1], rsend.at[1], rrecv.at[1], at_x(left))
    direct_r = remote(rs_send.at[2], rs_arr.at[0], rsend.at[2], rrecv.at[2], at_x(right))
    direct_l = remote(rs_send.at[3], rs_arr.at[1], rsend.at[3], rrecv.at[3], at_x(left))
    sum_r = remote(rs_send.at[4], rs_arr.at[2], rsend.at[4], rrecv.at[4], at_x(right))
    sum_l = remote(rs_send.at[5], rs_arr.at[3], rsend.at[5], rrecv.at[5], at_x(left))
    fill(rs_send.at[0], across, 0)
    relay_r.start()
    fill(rs_send.at[1], across, 1024)
    relay_l.start()
    fill(rs_send.at[2], right, 1024)
    direct_r.start()
    fill(rs_send.at[3], left, 0)
    direct_l.start()
    for j in range(2):
        rs_hold[0, :, j * 512 : (j + 1) * 512] = block(right, j * 512, 512)
    for j in range(2):
        rs_hold[1, :, j * 512 : (j + 1) * 512] = block(left, 1024 + j * 512, 512)
    relay_r.wait_recv()
    rs_send[4] = (rs_hold[0] + rs_relay[0].astype(F32)).astype(BF16)
    sum_r.start()
    relay_l.wait_recv()
    rs_send[5] = (rs_hold[1] + rs_relay[1].astype(F32)).astype(BF16)
    sum_l.start()
    for j in range(4):
        rs_own[:, j * 512 : (j + 1) * 512] = block(xx, j * 512, 512)
    direct_r.wait_recv()
    direct_l.wait_recv()
    sum_r.wait_recv()
    sum_l.wait_recv()
    out[:, 0:1024] = (rs_own[:, 0:1024] + rs_arr[1].astype(F32) + rs_arr[2].astype(F32)).astype(BF16)
    out[:, 1024:2048] = (rs_own[:, 1024:2048] + rs_arr[0].astype(F32) + rs_arr[3].astype(F32)).astype(BF16)

    swap.wait_send()

    @pl.when(core == 1)
    def _():
        halo0.wait_send()
        halo1.wait_send()

    for o in range(8):
        @pl.when(2 * o + core != chip)
        def _(o=o):
            to_owner(o).wait_send()

    @pl.when(owns)
    def _():
        for i in range(CHIPS):
            @pl.when(i != chip)
            def _(i=i):
                give(i).wait_send()

    n_swap.wait_send()
    for cp in (relay_r, relay_l, direct_r, direct_l, sum_r, sum_l):
        cp.wait_send()


def on_device(*args):
    any_space = pl.BlockSpec(memory_space=pl.ANY)
    vmem = pl.BlockSpec(memory_space=pltpu.VMEM)
    smem = pl.BlockSpec(memory_space=pltpu.SMEM)
    dma = pltpu.SemaphoreType.DMA
    return pl.pallas_call(
        kernel,
        out_shape=jax.ShapeDtypeStruct((64, DM), BF16),
        in_specs=[any_space] * 7 + [vmem] * 3 + [smem] * 3 + [vmem] + [any_space] * 2,
        out_specs=vmem,
        scratch_shapes=[
            pltpu.VMEM((HALO + ROWS, DM), BF16),
            pltpu.VMEM((6, DM, 256), BF16),
            pltpu.VMEM((DM, 8), BF16),
            pltpu.VMEM((DM, 8), BF16),
            pltpu.VMEM((1024, DM), BF16),
            pltpu.VMEM((128, 128), F32),
            pltpu.VMEM((4, HALO + ROWS, 256), F32),
            pltpu.VMEM((ROWS, 256), BF16),
            pltpu.VMEM((ROWS, 256), BF16),
            pltpu.VMEM((ROWS, 512), F32),
            pltpu.VMEM((ROWS, 512), F32),
            pltpu.VMEM((NC, CH, 128), F32),
            pltpu.VMEM((NC, 8, CH), F32),
            pltpu.VMEM((NC, CH, 128), F32),
            pltpu.VMEM((8, CH, 256), BF16),
            pltpu.VMEM((8, CH, 256), BF16),
            pltpu.VMEM((16, CH, CH), BF16),
            pltpu.VMEM((16, CH, 256), BF16),
            pltpu.VMEM((16, 128, 256), F32),
            pltpu.VMEM((16, 128, 256), BF16),
            pltpu.VMEM((NC, 8, 128), F32),
            pltpu.VMEM((ROWS, 512), BF16),
            pltpu.VMEM((ROWS, 512), F32),
            pltpu.VMEM((8, MSG, 128), BF16),
            pltpu.VMEM((CHIPS, MSG, 128), BF16),
            pltpu.VMEM((CHIPS, 64, 128), BF16),
            pltpu.VMEM((8, 64, 128), BF16),
            pltpu.VMEM((OWN, 512), BF16),
            pltpu.VMEM((2, OWN, 512), BF16),
            pltpu.VMEM((6, 64, 1024), BF16),
            pltpu.VMEM((2, 64, 1024), BF16),
            pltpu.VMEM((4, 64, 1024), BF16),
            pltpu.VMEM((64, DM), F32),
            pltpu.VMEM((2, 64, 1024), F32),
            dma((5,)),
            dma((6,)),
            dma((2,)),
            dma((3,)),
            dma((8,)),
            dma((CHIPS,)),
            dma((CHIPS,)),
            dma((8,)),
            dma((2,)),
            dma((6,)),
            dma((6,)),
        ],
        compiler_params=pltpu.CompilerParams(
            collective_id=0, has_side_effects=True, vmem_limit_bytes=56 * 1024 * 1024
        ),
    )(*args)


def solution(mesh):
    placed = (
        P("seq", None),
        P(None, "head"),
        P(None, "head"),
        P(None, "head"),
        P(None, "head"),
        P(None, "head"),
        P(None, "head"),
        P(None, "head"),
        P(None, "head"),
        P(None, "head"),
        P("head"),
        P("head"),
        P("head"),
        P(),
        P("head", None),
        P("head", None, None),
    )
    return jax.shard_map(
        on_device, mesh=mesh, in_specs=placed, out_specs=P(("seq", "head"), None), check_vma=False
    )
```

```python
import jax
import jax.numpy as jnp
from jax import lax
from jax.experimental import pallas as pl
from jax.experimental.pallas import tpu as pltpu
from jax.sharding import PartitionSpec as P

MESH = pl.DeviceIdType.MESH
F32 = jnp.float32
BF16 = jnp.bfloat16
HALO = 16
OWN = 256
ROWS = 512
DM = 2048
CH = 128
NC = ROWS // CH
HEADS = 4
CHIPS = 16
MSG = 272
LAST = CHIPS - 1
OWNERS = ((3, 6, 9, 12), (2, 5, 10, 13))


def dot(a, b):
    return jnp.dot(a, b, preferred_element_type=F32)


def dot_nt(a, b):
    return lax.dot_general(a, b, (((1,), (1,)), ((), ())), preferred_element_type=F32)


def silu(u):
    return u * jax.nn.sigmoid(u)


def kernel(
    hidden, w_query, w_key, w_value, w_gate_z, w_decay, w_beta, conv_query, conv_key, conv_value,
    decay_log, decay_bias, beta_bias, norm_gain, w_out, state_in,
    out,
    hid, wbuf, wo, st0, raw0, raw1, raw2, raw3, qs, ks, vs, zs, cum, cumt, low, tri, att, uw, ee, sb, ab,
    reach, outloc, send, recv, step_out, entering, nsend, nfull, rs_send, rs_relay, rs_arr, rs_own, rs_hold,
    lsem, wsem, xsem, hsem, msend, mrecv, osend, orecv, nsem, rsend, rrecv, ready,
):
    seq = lax.axis_index("seq")
    xx = lax.axis_index("head")
    chip = seq // 2
    core = seq % 2
    other = 1 - core
    partner = (chip * 2 + other, xx)
    nxt = lax.rem(chip + 1, CHIPS)
    prv = lax.rem(chip + CHIPS - 1, CHIPS)
    right = lax.rem(xx + 1, 4)
    left = lax.rem(xx + 3, 4)
    across = lax.rem(xx + 2, 4)

    def at_x(x):
        return (seq, x)

    def local(src, dst, sem):
        return pltpu.make_async_copy(src, dst, sem)

    def remote(src, dst, s_sem, r_sem, device):
        return pltpu.make_async_remote_copy(
            src_ref=src, dst_ref=dst, send_sem=s_sem, recv_sem=r_sem, device_id=device, device_id_type=MESH
        )

    col256 = pl.ds(pl.multiple_of(core * 256, 256), 256)
    owners = [lax.select(core == 0, OWNERS[0][j], OWNERS[1][j]) for j in range(HEADS)]
    my_head = jnp.int32(0)
    owns = owners[0] == chip
    for j in range(1, HEADS):
        my_head = lax.select(owners[j] == chip, j, my_head)
        owns = owns | (owners[j] == chip)
    owns_one = lax.select(owns, 1, 0)

    def chunk_rows(c):
        return pl.ds(c * CH, CH)

    def run(step):
        for c in range(NC):
            step(c, 0)

    own_copy = local(hidden, hid.at[pl.ds(0, OWN), :], lsem.at[0])
    own_copy.start()
    w_copies = [
        local(w_query.at[:, col256], wbuf.at[0], wsem.at[0]),
        local(w_key.at[:, col256], wbuf.at[1], wsem.at[1]),
    ]
    for i in range(2):
        cols = pl.ds(pl.multiple_of(core * 512 + i * 256, 256), 256)
        w_copies.append(local(w_value.at[:, cols], wbuf.at[2 + i], wsem.at[2 + i]))
    for i in range(2):
        cols = pl.ds(pl.multiple_of(core * 512 + i * 256, 256), 256)
        w_copies.append(local(w_gate_z.at[:, cols], wbuf.at[4 + i], wsem.at[4 + i]))
    for cp in w_copies[:4]:
        cp.start()
    st_copy = local(state_in.at[core * HEADS + my_head], st0, lsem.at[3])
    wo_copy = local(w_out, wo, lsem.at[4])

    barrier = pltpu.get_barrier_semaphore()

    def greet(device):
        pl.semaphore_signal(barrier, inc=1, device_id=device, device_id_type=MESH)

    greet(partner)
    greet(at_x(right))
    greet(at_x(left))

    @pl.when(chip > 0)
    def _():
        greet((prv * 2 + 1, xx))

    @pl.when(owns)
    def _():
        def greet_chip(k, carry):
            greet((lax.rem(chip + k, CHIPS) * 2 + core, xx))
            return carry

        lax.fori_loop(1, CHIPS, greet_chip, 0)

    sends_halo = (core == 1) & (chip < LAST)
    pl.semaphore_wait(barrier, 3 + HEADS - owns_one + lax.select(sends_halo, 2, 0))

    swap = remote(hidden, hid.at[pl.ds(OWN, OWN), :], xsem.at[0], xsem.at[1], partner)
    swap.start()
    tail = hidden.at[pl.ds(OWN - HALO, HALO), :]
    halo_at = hid.at[pl.ds(ROWS, HALO), :]
    halo0 = remote(tail, halo_at, hsem.at[0], hsem.at[2], (nxt * 2, xx))
    halo1 = remote(tail, halo_at, hsem.at[1], hsem.at[2], (nxt * 2 + 1, xx))

    @pl.when(sends_halo)
    def _():
        halo0.start()
        halo1.start()

    for j in range(HEADS):
        @pl.when(owners[j] != chip)
        def _(j=j):
            pl.semaphore_signal(
                ready.at[chip], inc=1, device_id=(owners[j] * 2 + core, xx), device_id_type=MESH
            )

    raws = (raw0, raw1, raw2, raw3)
    rows_own = pl.ds(pl.multiple_of(HALO + core * OWN, 16), OWN)
    rows_other = pl.ds(pl.multiple_of(HALO + other * OWN, 16), OWN)
    own_copy.wait()
    for b in range(4):
        w_copies[b].wait()
        raws[b][rows_own, :] = dot(hid[0:OWN, :], wbuf[b]).astype(BF16).astype(F32)
    for cp in w_copies[4:]:
        cp.start()
    st_copy.start()
    wo_copy.start()
    swap.wait_recv()

    @pl.when(chip > 0)
    def _():
        halo0.wait_recv()

    @pl.when(chip == 0)
    def _():
        hid[ROWS : ROWS + HALO, :] = jnp.zeros((HALO, DM), BF16)

    taps_of = (
        lambda: conv_query[:, col256].astype(F32),
        lambda: conv_key[:, col256].astype(F32),
        lambda: conv_value[:, pl.ds(pl.multiple_of(core * 512, 256), 256)].astype(F32),
        lambda: conv_value[:, pl.ds(pl.multiple_of(core * 512 + 256, 256), 256)].astype(F32),
    )
    for b in range(4):
        raw = raws[b]
        rest = dot(hid[OWN : ROWS + HALO, :], wbuf[b]).astype(BF16).astype(F32)
        raw[rows_other, :] = rest[:OWN]
        raw[0:HALO, :] = rest[OWN:]
        taps = taps_of[b]()
        for t in range(NC):
            pre = jnp.zeros((CH, 256), F32)
            for i in range(4):
                pre = pre + taps[i : i + 1, :] * raw[pl.ds(HALO - 3 + i + t * CH, CH), :]
            act = silu(pre)
            r = pl.ds(t * CH, CH)
            if b < 2:
                for g in range(2):
                    a = act[:, g * 128 : (g + 1) * 128]
                    n = a * lax.rsqrt(jnp.sum(a * a, axis=-1, keepdims=True) + 1e-6)
                    if b == 0:
                        qs[r, g * 128 : (g + 1) * 128] = (n * 128 ** (-0.5)).astype(BF16)
                    else:
                        ks[r, g * 128 : (g + 1) * 128] = n.astype(BF16)
            else:
                vs[r, (b - 2) * 256 : (b - 1) * 256] = act

    head_row = lax.broadcasted_iota(jnp.int32, (HEADS, 1), 0)

    def column_of(ref):
        v = jnp.zeros((HEADS, 1), F32)
        for h in range(HEADS):
            v = jnp.where(head_row == h, ref[core * HEADS + h], v)
        return v

    rate = -jnp.exp(column_of(decay_log))
    ti = lax.broadcasted_iota(jnp.int32, (CH, CH), 0)
    tj = lax.broadcasted_iota(jnp.int32, (CH, CH), 1)
    incl = ti >= tj
    ones_up = jnp.where(ti <= tj, 1.0, 0.0).astype(F32)
    w_gates = jnp.concatenate([w_decay[...].astype(F32), w_beta[...].astype(F32)], 0).astype(BF16)
    lg = dot_nt(w_gates, hid[0:ROWS, :])
    logits = jnp.concatenate(
        [jnp.where(core == 0, lg[:, :OWN], lg[:, OWN:]), jnp.where(core == 0, lg[:, OWN:], lg[:, :OWN])], 1
    )
    u = jnp.where(core == 0, logits[0:4], logits[4:8]) + column_of(decay_bias)
    glog = rate * (jnp.maximum(u, 0.0) + jnp.log1p(jnp.exp(-jnp.abs(u))))
    strength = jax.nn.sigmoid(jnp.where(core == 0, logits[8:12], logits[12:16]) + column_of(beta_bias))
    pad4 = jnp.zeros((4, CH), F32)
    for t in range(NC):
        cols = slice(t * CH, (t + 1) * CH)
        g8 = jnp.concatenate([glog[:, cols], pad4], 0)
        cr8 = jnp.dot(g8, ones_up, precision=lax.Precision.HIGHEST, preferred_element_type=F32)
        cumt[t] = cr8
        stacked = jnp.concatenate([cr8, strength[:, cols], jnp.zeros((CH - 12, CH), F32)], 0)
        cum[t] = stacked.T

    def systems(c, carry):
        r = chunk_rows(c)
        cc_all = cum[c]
        cr_all = cumt[c]
        for g in range(2):
            k = ks[r, g * 128 : (g + 1) * 128]
            q = qs[r, g * 128 : (g + 1) * 128]
            both = dot_nt(jnp.concatenate([k, q], 0), k)
            kk, qk = both[:CH], both[CH:]
            for e in range(2):
                h = 2 * g + e
                diff = cc_all[:, h : h + 1] - cr_all[h : h + 1, :]
                ratio = jnp.exp(jnp.where(incl, diff, -1e30))
                lo = jnp.where(ti > tj, cc_all[:, 8 + h : 9 + h] * ratio * kk, 0.0)
                low[c * 2 + g, :, e * 128 : (e + 1) * 128] = lo.astype(BF16)
                att[c * 4 + h] = (ratio * qk).astype(BF16)
                tri[c * 2 + g, :, e * 128 : (e + 1) * 128] = jnp.where(
                    ti == tj, 1.0, jnp.where((ti ^ tj) == 1, -lo, 0.0)
                ).astype(BF16)
        return carry

    run(systems)

    z128 = jnp.zeros((CH, CH), BF16)

    def pair_diag(m):
        return jnp.concatenate(
            [jnp.concatenate([m[:, :128], z128], 1), jnp.concatenate([z128, m[:, 128:]], 1)], 0
        )

    pi = lax.broadcasted_iota(jnp.int32, (CH, 256), 0)
    pj = lax.broadcasted_iota(jnp.int32, (CH, 256), 1) % 128
    pxor = pi ^ pj

    def double(level, size):
        mask = (pxor >= size) & (pxor < 2 * size)
        prods = []
        for p in range(8):
            lm = jnp.where(mask, low[p].astype(F32), 0.0).astype(BF16)
            prods.append(dot(tri[p], pair_diag(lm)).astype(BF16))
        for p in range(8):
            t_old = tri[p]
            y = dot(prods[p], pair_diag(t_old))
            tri[p] = (t_old.astype(F32) - y).astype(BF16)
        return size * 2

    lax.fori_loop(0, 6, double, jnp.int32(2))

    def unit(c, carry):
        r = chunk_rows(c)
        cc_all = cum[c]
        cr_all = cumt[c]
        for g in range(2):
            k = ks[r, g * 128 : (g + 1) * 128].astype(F32)
            kt = k.T
            for e in range(2):
                h = 2 * g + e
                be = cc_all[:, 8 + h : 9 + h]
                cc = cc_all[:, h : h + 1]
                cr = cr_all[h : h + 1, :]
                tail_w = jnp.exp(cr[:, 127:128] - cr)
                rhs = jnp.concatenate([be * vs[r, h * 128 : (h + 1) * 128], (be * jnp.exp(cc)) * k], 1)
                u = dot(tri[c * 2 + g, :, e * 128 : (e + 1) * 128], rhs.astype(BF16)).astype(BF16)
                uw[c * 4 + h] = u
                ee[c * 4 + h] = dot((kt * tail_w).astype(BF16), u)
        return carry

    run(unit)

    row16 = lax.broadcasted_iota(jnp.int32, (16, 128), 0)
    s_cur, b_cur, a_cur = [], [], []
    for h in range(HEADS):
        e0 = ee[h]
        s_cur.append(e0[:, :128])
        b_cur.append(-e0[:, 128:])
        a_cur.append(jnp.exp(cumt[0, h : h + 1, 127:128]))
        sb[h] = jnp.zeros((128, 256), BF16)
        ab[0, h : h + 1, :] = jnp.ones((1, 128), F32)
    for c in range(1, NC):
        for h in range(HEADS):
            s, bm, a = s_cur[h], b_cur[h], a_cur[h]
            packed = jnp.concatenate([s, bm], 1).astype(BF16)
            sb[c * 4 + h] = packed
            ab[c, h : h + 1, :] = jnp.broadcast_to(a, (1, 128))
            e_c = ee[c * 4 + h]
            m_c = e_c[:, 128:]
            p = dot(m_c.astype(BF16), packed)
            al = jnp.exp(cumt[c, h : h + 1, 127:128])
            s_cur[h] = al * s - p[:, :128] + e_c[:, :128]
            b_cur[h] = al * bm - a * m_c - p[:, 128:]
            a_cur[h] = a * al
    for h in range(HEADS):
        bt = b_cur[h].T.astype(BF16)
        s_t = s_cur[h].T.astype(BF16)
        a_full = jnp.broadcast_to(a_cur[h], (16, 128))
        a_hi = a_full.astype(BF16).astype(F32)
        a_rows = jnp.where(row16 < 8, a_hi, a_full - a_hi).astype(BF16)
        send[h, 0:128, :] = bt
        send[h, 128:256, :] = s_t
        send[h, 256:272, :] = a_rows

    def to_owner(j):
        return remote(send.at[j], recv.at[chip], msend.at[j], mrecv.at[chip], (owners[j] * 2 + core, xx))

    for j in range(HEADS):
        @pl.when((owners[j] != chip) & (chip < LAST))
        def _(j=j):
            to_owner(j).start()

        @pl.when(owners[j] == chip)
        def _(j=j):
            recv[chip] = send[j]

    def local_part(c, carry):
        r = chunk_rows(c)
        cc_all = cum[c]
        a_all = ab[c]
        for h in range(HEADS):
            g = h // 2
            q = qs[r, g * 128 : (g + 1) * 128].astype(F32)
            o = dot(att[c * 4 + h], uw[c * 4 + h])
            qeff = jnp.exp(cc_all[:, h : h + 1]) * q - o[:, 128:]
            rr = dot(qeff.astype(BF16), sb[c * 4 + h])
            outloc[r, h * 128 : (h + 1) * 128] = o[:, :128] + rr[:, :128]
            reach[r, h * 128 : (h + 1) * 128] = (a_all[h : h + 1, :] * qeff + rr[:, 128:]).astype(BF16)
        return carry

    run(local_part)

    for b in range(2):
        w_copies[4 + b].wait()
    gain = jnp.concatenate([norm_gain[...].reshape(1, 128)] * 2, 1)

    def gate_rows(t, carry):
        r = chunk_rows(t)
        h_rows = hid[chunk_rows(t), :]
        for b in range(2):
            zs[r, b * 256 : (b + 1) * 256] = silu(dot(h_rows, wbuf[4 + b])) * gain
        return carry

    run(gate_rows)

    st_copy.wait()

    def give(i):
        return remote(step_out.at[i], entering.at[my_head], osend.at[i], orecv.at[my_head], (i * 2 + core, xx))

    @pl.when(owns)
    def _():
        s = st0[...].T
        for i in range(CHIPS):
            sbf = s.astype(BF16)
            step_out[i] = sbf

            @pl.when(i != chip)
            def _(i=i):
                pl.semaphore_wait(ready.at[i], 1)
                give(i).start()

            if i < LAST:
                @pl.when(i != chip)
                def _(i=i):
                    remote(send.at[0], recv.at[i], msend.at[0], mrecv.at[i], partner).wait_recv()

                a = recv[i, 256:272, :].astype(F32)
                s = (a[0:1, :] + a[8:9, :]) * s + dot(sbf, recv[i, 0:128, :]) + recv[i, 128:256, :].astype(F32)
        entering[my_head] = step_out[chip]

    for j in range(HEADS):
        @pl.when(owners[j] != chip)
        def _(j=j):
            remote(step_out.at[0], entering.at[j], osend.at[0], orecv.at[j], partner).wait_recv()

    def finish(base, z_base, put):
        for t in range(2):
            r = pl.ds(pl.multiple_of(base + t * CH, CH), CH)
            for h in range(HEADS):
                cols = slice(h * 128, (h + 1) * 128)
                s_t = entering[h]
                o = outloc[r, cols] + dot_nt(reach[r, cols], s_t)
                n = o * lax.rsqrt(jnp.mean(o * o, axis=-1, keepdims=True) + 1e-6) * zs[z_base + t * CH : z_base + (t + 1) * CH, cols]
                put(t, cols, n.astype(BF16))

    def put_send(t, cols, v):
        nsend[t * CH : (t + 1) * CH, cols] = v

    def put_own(t, cols, v):
        nfull[core, t * CH : (t + 1) * CH, cols] = v

    finish(other * OWN, OWN, put_send)
    n_swap = remote(nsend, nfull.at[core], nsem.at[0], nsem.at[1], partner)
    n_swap.start()
    finish(core * OWN, 0, put_own)
    wo_copy.wait()
    n_swap.wait_recv()

    def block(x, n0, width):
        r = pl.ds(pl.multiple_of(x * 64, 64), 64)
        cols = slice(n0, n0 + width)
        return dot(nfull[0, r, :], wo[0:512, cols]) + dot(nfull[1, r, :], wo[512:1024, cols])

    def fill(dst, x, n0):
        for j in range(2):
            dst[:, j * 512 : (j + 1) * 512] = block(x, n0 + j * 512, 512).astype(BF16)

    relay_r = remote(rs_send.at[0], rs_relay.at[0], rsend.at[0], rrecv.at[0], at_x(right))
    relay_l = remote(rs_send.at[1], rs_relay.at[1], rsend.at[1], rrecv.at[1], at_x(left))
    direct_r = remote(rs_send.at[2], rs_arr.at[0], rsend.at[2], rrecv.at[2], at_x(right))
    direct_l = remote(rs_send.at[3], rs_arr.at[1], rsend.at[3], rrecv.at[3], at_x(left))
    sum_r = remote(rs_send.at[4], rs_arr.at[2], rsend.at[4], rrecv.at[4], at_x(right))
    sum_l = remote(rs_send.at[5], rs_arr.at[3], rsend.at[5], rrecv.at[5], at_x(left))
    fill(rs_send.at[0], across, 0)
    relay_r.start()
    fill(rs_send.at[1], across, 1024)
    relay_l.start()
    fill(rs_send.at[2], right, 1024)
    direct_r.start()
    fill(rs_send.at[3], left, 0)
    direct_l.start()
    for j in range(2):
        rs_hold[0, :, j * 512 : (j + 1) * 512] = block(right, j * 512, 512)
    for j in range(2):
        rs_hold[1, :, j * 512 : (j + 1) * 512] = block(left, 1024 + j * 512, 512)
    relay_r.wait_recv()
    rs_send[4] = (rs_hold[0] + rs_relay[0].astype(F32)).astype(BF16)
    sum_r.start()
    relay_l.wait_recv()
    rs_send[5] = (rs_hold[1] + rs_relay[1].astype(F32)).astype(BF16)
    sum_l.start()
    for j in range(4):
        rs_own[:, j * 512 : (j + 1) * 512] = block(xx, j * 512, 512)
    direct_r.wait_recv()
    direct_l.wait_recv()
    sum_r.wait_recv()
    sum_l.wait_recv()
    out[:, 0:1024] = (rs_own[:, 0:1024] + rs_arr[1].astype(F32) + rs_arr[2].astype(F32)).astype(BF16)
    out[:, 1024:2048] = (rs_own[:, 1024:2048] + rs_arr[0].astype(F32) + rs_arr[3].astype(F32)).astype(BF16)

    swap.wait_send()

    @pl.when(sends_halo)
    def _():
        halo0.wait_send()
        halo1.wait_send()

    for j in range(HEADS):
        @pl.when((owners[j] != chip) & (chip < LAST))
        def _(j=j):
            to_owner(j).wait_send()

    @pl.when(owns)
    def _():
        for i in range(CHIPS):
            @pl.when(i != chip)
            def _(i=i):
                give(i).wait_send()

    n_swap.wait_send()
    for cp in (relay_r, relay_l, direct_r, direct_l, sum_r, sum_l):
        cp.wait_send()


def on_device(*args):
    any_space = pl.BlockSpec(memory_space=pl.ANY)
    vmem = pl.BlockSpec(memory_space=pltpu.VMEM)
    smem = pl.BlockSpec(memory_space=pltpu.SMEM)
    dma = pltpu.SemaphoreType.DMA
    return pl.pallas_call(
        kernel,
        out_shape=jax.ShapeDtypeStruct((64, DM), BF16),
        in_specs=[any_space] * 5 + [vmem] * 5 + [smem] * 3 + [vmem] + [any_space] * 2,
        out_specs=vmem,
        scratch_shapes=[
            pltpu.VMEM((HALO + ROWS, DM), BF16),
            pltpu.VMEM((6, DM, 256), BF16),
            pltpu.VMEM((1024, DM), BF16),
            pltpu.VMEM((128, 128), F32),
            *[pltpu.VMEM((HALO + ROWS, 256), F32)] * 4,
            pltpu.VMEM((ROWS, 256), BF16),
            pltpu.VMEM((ROWS, 256), BF16),
            pltpu.VMEM((ROWS, 512), F32),
            pltpu.VMEM((ROWS, 512), F32),
            pltpu.VMEM((NC, CH, 128), F32),
            pltpu.VMEM((NC, 8, CH), F32),
            pltpu.VMEM((8, CH, 256), BF16),
            pltpu.VMEM((8, CH, 256), BF16),
            pltpu.VMEM((16, CH, CH), BF16),
            pltpu.VMEM((16, CH, 256), BF16),
            pltpu.VMEM((16, 128, 256), F32),
            pltpu.VMEM((16, 128, 256), BF16),
            pltpu.VMEM((NC, 8, 128), F32),
            pltpu.VMEM((ROWS, 512), BF16),
            pltpu.VMEM((ROWS, 512), F32),
            pltpu.VMEM((HEADS, MSG, 128), BF16),
            pltpu.VMEM((CHIPS, MSG, 128), BF16),
            pltpu.VMEM((CHIPS, 128, 128), BF16),
            pltpu.VMEM((HEADS, 128, 128), BF16),
            pltpu.VMEM((OWN, 512), BF16),
            pltpu.VMEM((2, OWN, 512), BF16),
            pltpu.VMEM((6, 64, 1024), BF16),
            pltpu.VMEM((2, 64, 1024), BF16),
            pltpu.VMEM((4, 64, 1024), BF16),
            pltpu.VMEM((64, DM), F32),
            pltpu.VMEM((2, 64, 1024), F32),
            dma((5,)),
            dma((6,)),
            dma((2,)),
            dma((3,)),
            dma((HEADS,)),
            dma((CHIPS,)),
            dma((CHIPS,)),
            dma((HEADS,)),
            dma((2,)),
            dma((6,)),
            dma((6,)),
            pltpu.SemaphoreType.REGULAR((CHIPS,)),
        ],
        compiler_params=pltpu.CompilerParams(
            collective_id=0, has_side_effects=True, vmem_limit_bytes=56 * 1024 * 1024
        ),
    )(*args[:5], args[5].T, args[6].T, *args[7:])


def solution(mesh):
    placed = (
        P("seq", None),
        P(None, "head"),
        P(None, "head"),
        P(None, "head"),
        P(None, "head"),
        P(None, "head"),
        P(None, "head"),
        P(None, "head"),
        P(None, "head"),
        P(None, "head"),
        P("head"),
        P("head"),
        P("head"),
        P(),
        P("head", None),
        P("head", None, None),
    )
    return jax.shard_map(
        on_device, mesh=mesh, in_specs=placed, out_specs=P(("seq", "head"), None), check_vma=False
    )
```

```python
import jax
import jax.numpy as jnp
from jax import lax
from jax.experimental import pallas as pl
from jax.experimental.pallas import tpu as pltpu
from jax.sharding import PartitionSpec as P

MESH = pl.DeviceIdType.MESH
F32 = jnp.float32
BF16 = jnp.bfloat16
HALO = 16
OWN = 256
ROWS = 512
DM = 2048
CH = 128
NC = ROWS // CH
HEADS = 4
CHIPS = 16
MSG = 272
LAST = CHIPS - 1
LINE = 4


def dot(a, b):
    return jnp.dot(a, b, preferred_element_type=F32)


def dot_nt(a, b):
    return lax.dot_general(a, b, (((1,), (1,)), ((), ())), preferred_element_type=F32)


def silu(u):
    return u * jax.nn.sigmoid(u)


def kernel(
    hidden, w_query, w_key, w_value, w_gate_z, w_decay, w_beta, conv_query, conv_key, conv_value,
    decay_log, decay_bias, beta_bias, norm_gain, w_out, state_in,
    out,
    hid, wbuf, wo, st0, raw0, raw1, raw2, raw3, qs, ks, vs, zs, cum, cumt, low, tri, att, uw, ee, sb, ab,
    reach, outloc, send, recv, tsend, trecv, pre_x, pre_a, step_out, entering, nsend, nfull, rs_send, rs_relay, rs_arr, rs_own, rs_hold,
    lsem, wsem, xsem, hsem, msend, mrecv, tsems, osend, orecv, nsem, rsend, rrecv, ready,
):
    seq = lax.axis_index("seq")
    xx = lax.axis_index("head")
    chip = seq // 2
    core = seq % 2
    other = 1 - core
    partner = (chip * 2 + other, xx)
    nxt = lax.rem(chip + 1, CHIPS)
    prv = lax.rem(chip + CHIPS - 1, CHIPS)
    right = lax.rem(xx + 1, 4)
    left = lax.rem(xx + 3, 4)
    across = lax.rem(xx + 2, 4)

    def at_x(x):
        return (seq, x)

    def local(src, dst, sem):
        return pltpu.make_async_copy(src, dst, sem)

    def remote(src, dst, s_sem, r_sem, device):
        return pltpu.make_async_remote_copy(
            src_ref=src, dst_ref=dst, send_sem=s_sem, recv_sem=r_sem, device_id=device, device_id_type=MESH
        )

    col256 = pl.ds(pl.multiple_of(core * 256, 256), 256)
    zz = lax.rem(chip, LINE)
    yy = chip // LINE

    def at_z(z):
        return ((yy * LINE + z) * 2 + core, xx)

    def at_y(y):
        return ((y * LINE + zz) * 2 + core, xx)

    def chunk_rows(c):
        return pl.ds(c * CH, CH)

    def run(step):
        for c in range(NC):
            step(c, 0)

    own_copy = local(hidden, hid.at[pl.ds(0, OWN), :], lsem.at[0])
    own_copy.start()
    w_copies = [
        local(w_query.at[:, col256], wbuf.at[0], wsem.at[0]),
        local(w_key.at[:, col256], wbuf.at[1], wsem.at[1]),
    ]
    for i in range(2):
        cols = pl.ds(pl.multiple_of(core * 512 + i * 256, 256), 256)
        w_copies.append(local(w_value.at[:, cols], wbuf.at[2 + i], wsem.at[2 + i]))
    for i in range(2):
        cols = pl.ds(pl.multiple_of(core * 512 + i * 256, 256), 256)
        w_copies.append(local(w_gate_z.at[:, cols], wbuf.at[4 + i], wsem.at[4 + i]))
    for cp in w_copies[:4]:
        cp.start()
    st_copy = local(state_in.at[core * HEADS + zz], st0, lsem.at[3])
    wo_copy = local(w_out, wo, lsem.at[4])

    barrier = pltpu.get_barrier_semaphore()

    def greet(device):
        pl.semaphore_signal(barrier, inc=1, device_id=device, device_id_type=MESH)

    greet(partner)
    greet(at_x(right))
    greet(at_x(left))

    @pl.when(chip > 0)
    def _():
        greet((prv * 2 + 1, xx))

    for n in range(1, LINE):
        @pl.when(n > zz)
        def _(n=n):
            greet(at_z(n))

        @pl.when(n > yy)
        def _(n=n):
            greet(at_y(n))

    sends_halo = (core == 1) & (chip < LAST)
    pl.semaphore_wait(barrier, 3 + zz + yy + lax.select(sends_halo, 2, 0))

    swaps = [
        remote(
            hidden.at[pl.ds(i * 64, 64), :], hid.at[pl.ds(OWN + i * 64, 64), :], xsem.at[i], xsem.at[4 + i], partner
        )
        for i in range(4)
    ]
    for cp in swaps:
        cp.start()
    tail = hidden.at[pl.ds(OWN - HALO, HALO), :]
    halo_at = hid.at[pl.ds(ROWS, HALO), :]
    halo0 = remote(tail, halo_at, hsem.at[0], hsem.at[2], (nxt * 2, xx))
    halo1 = remote(tail, halo_at, hsem.at[1], hsem.at[2], (nxt * 2 + 1, xx))

    @pl.when(sends_halo)
    def _():
        halo0.start()
        halo1.start()

    for n in range(LINE - 1):
        @pl.when(n < zz)
        def _(n=n):
            pl.semaphore_signal(ready.at[zz], inc=1, device_id=at_z(n), device_id_type=MESH)

        @pl.when(n < yy)
        def _(n=n):
            pl.semaphore_signal(ready.at[LINE + yy], inc=1, device_id=at_y(n), device_id_type=MESH)

    raws = (raw0, raw1, raw2, raw3)
    rows_own = pl.ds(pl.multiple_of(HALO + core * OWN, 16), OWN)
    rows_other = pl.ds(pl.multiple_of(HALO + other * OWN, 16), OWN)
    own_copy.wait()
    for b in range(4):
        w_copies[b].wait()
        raws[b][rows_own, :] = dot(hid[0:OWN, :], wbuf[b]).astype(BF16).astype(F32)
    for cp in w_copies[4:]:
        cp.start()
    st_copy.start()
    wo_copy.start()
    for cp in swaps:
        cp.wait_recv()

    @pl.when(chip > 0)
    def _():
        halo0.wait_recv()

    @pl.when(chip == 0)
    def _():
        hid[ROWS : ROWS + HALO, :] = jnp.zeros((HALO, DM), BF16)

    taps_of = (
        lambda: conv_query[:, col256].astype(F32),
        lambda: conv_key[:, col256].astype(F32),
        lambda: conv_value[:, pl.ds(pl.multiple_of(core * 512, 256), 256)].astype(F32),
        lambda: conv_value[:, pl.ds(pl.multiple_of(core * 512 + 256, 256), 256)].astype(F32),
    )
    for b in range(4):
        raw = raws[b]
        rest = dot(hid[OWN : ROWS + HALO, :], wbuf[b]).astype(BF16).astype(F32)
        raw[rows_other, :] = rest[:OWN]
        raw[0:HALO, :] = rest[OWN:]
        taps = taps_of[b]()
        for t in range(NC):
            pre = jnp.zeros((CH, 256), F32)
            for i in range(4):
                pre = pre + taps[i : i + 1, :] * raw[pl.ds(HALO - 3 + i + t * CH, CH), :]
            act = silu(pre)
            r = pl.ds(t * CH, CH)
            if b < 2:
                for g in range(2):
                    a = act[:, g * 128 : (g + 1) * 128]
                    n = a * lax.rsqrt(jnp.sum(a * a, axis=-1, keepdims=True) + 1e-6)
                    if b == 0:
                        qs[r, g * 128 : (g + 1) * 128] = (n * 128 ** (-0.5)).astype(BF16)
                    else:
                        ks[r, g * 128 : (g + 1) * 128] = n.astype(BF16)
            else:
                vs[r, (b - 2) * 256 : (b - 1) * 256] = act

    head_row = lax.broadcasted_iota(jnp.int32, (HEADS, 1), 0)

    def column_of(ref):
        v = jnp.zeros((HEADS, 1), F32)
        for h in range(HEADS):
            v = jnp.where(head_row == h, ref[core * HEADS + h], v)
        return v

    rate = -jnp.exp(column_of(decay_log))
    ti = lax.broadcasted_iota(jnp.int32, (CH, CH), 0)
    tj = lax.broadcasted_iota(jnp.int32, (CH, CH), 1)
    incl = ti >= tj
    ones_up = jnp.where(ti <= tj, 1.0, 0.0).astype(F32)
    w_gates = jnp.concatenate([w_decay[...].astype(F32), w_beta[...].astype(F32)], 0).astype(BF16)
    lg = dot_nt(w_gates, hid[0:ROWS, :])
    logits = jnp.concatenate(
        [jnp.where(core == 0, lg[:, :OWN], lg[:, OWN:]), jnp.where(core == 0, lg[:, OWN:], lg[:, :OWN])], 1
    )
    u = jnp.where(core == 0, logits[0:4], logits[4:8]) + column_of(decay_bias)
    glog = rate * (jnp.maximum(u, 0.0) + jnp.log1p(jnp.exp(-jnp.abs(u))))
    strength = jax.nn.sigmoid(jnp.where(core == 0, logits[8:12], logits[12:16]) + column_of(beta_bias))
    pad4 = jnp.zeros((4, CH), F32)
    for t in range(NC):
        cols = slice(t * CH, (t + 1) * CH)
        g8 = jnp.concatenate([glog[:, cols], pad4], 0)
        cr8 = jnp.dot(g8, ones_up, precision=lax.Precision.HIGHEST, preferred_element_type=F32)
        cumt[t] = cr8
        stacked = jnp.concatenate([cr8, strength[:, cols], jnp.zeros((CH - 12, CH), F32)], 0)
        cum[t] = stacked.T

    z128 = jnp.zeros((CH, CH), BF16)

    def pair_diag(m):
        return jnp.concatenate(
            [jnp.concatenate([m[:, :128], z128], 1), jnp.concatenate([z128, m[:, 128:]], 1)], 0
        )

    pi = lax.broadcasted_iota(jnp.int32, (CH, 256), 0)
    pj = lax.broadcasted_iota(jnp.int32, (CH, 256), 1) % 128
    pxor = pi ^ pj
    row16 = lax.broadcasted_iota(jnp.int32, (16, 128), 0)

    def systems(c, g):
        r = chunk_rows(c)
        cc_all = cum[c]
        cr_all = cumt[c]
        k = ks[r, g * 128 : (g + 1) * 128]
        q = qs[r, g * 128 : (g + 1) * 128]
        both = dot_nt(jnp.concatenate([k, q], 0), k)
        kk, qk = both[:CH], both[CH:]
        for e in range(2):
            h = 2 * g + e
            diff = cc_all[:, h : h + 1] - cr_all[h : h + 1, :]
            ratio = jnp.exp(jnp.where(incl, diff, -1e30))
            lo = jnp.where(ti > tj, cc_all[:, 8 + h : 9 + h] * ratio * kk, 0.0)
            low[c * 2 + g, :, e * 128 : (e + 1) * 128] = lo.astype(BF16)
            att[c * 4 + h] = (ratio * qk).astype(BF16)
            tri[c * 2 + g, :, e * 128 : (e + 1) * 128] = jnp.where(
                ti == tj, 1.0, jnp.where((ti ^ tj) == 1, -lo, 0.0)
            ).astype(BF16)

    def invert():
        pairs = range(2 * NC)

        def double(level, size):
            mask = (pxor >= size) & (pxor < 2 * size)
            prods = []
            for p in pairs:
                lm = jnp.where(mask, low[p].astype(F32), 0.0).astype(BF16)
                prods.append(dot(tri[p], pair_diag(lm)).astype(BF16))
            for p, prod in zip(pairs, prods):
                t_old = tri[p]
                y = dot(prod, pair_diag(t_old))
                tri[p] = (t_old.astype(F32) - y).astype(BF16)
            return size * 2

        lax.fori_loop(0, 6, double, jnp.int32(2))

    def unit(c, g):
        r = chunk_rows(c)
        cc_all = cum[c]
        cr_all = cumt[c]
        k = ks[r, g * 128 : (g + 1) * 128].astype(F32)
        kt = k.T
        for e in range(2):
            h = 2 * g + e
            be = cc_all[:, 8 + h : 9 + h]
            cc = cc_all[:, h : h + 1]
            cr = cr_all[h : h + 1, :]
            tail_w = jnp.exp(cr[:, 127:128] - cr)
            rhs = jnp.concatenate([be * vs[r, h * 128 : (h + 1) * 128], (be * jnp.exp(cc)) * k], 1)
            u = dot(tri[c * 2 + g, :, e * 128 : (e + 1) * 128], rhs.astype(BF16)).astype(BF16)
            uw[c * 4 + h] = u
            ee[c * 4 + h] = dot((kt * tail_w).astype(BF16), u)

    def map_of(heads):
        s_cur, b_cur, a_cur = {}, {}, {}
        for h in heads:
            e0 = ee[h]
            s_cur[h] = e0[:, :128]
            b_cur[h] = -e0[:, 128:]
            a_cur[h] = jnp.exp(cumt[0, h : h + 1, 127:128])
            sb[h] = jnp.zeros((128, 256), BF16)
            ab[0, h : h + 1, :] = jnp.ones((1, 128), F32)
        for c in range(1, NC):
            for h in heads:
                s, bm, a = s_cur[h], b_cur[h], a_cur[h]
                packed = jnp.concatenate([s, bm], 1).astype(BF16)
                sb[c * 4 + h] = packed
                ab[c, h : h + 1, :] = jnp.broadcast_to(a, (1, 128))
                e_c = ee[c * 4 + h]
                m_c = e_c[:, 128:]
                p = dot(m_c.astype(BF16), packed)
                al = jnp.exp(cumt[c, h : h + 1, 127:128])
                s_cur[h] = al * s - p[:, :128] + e_c[:, :128]
                b_cur[h] = al * bm - a * m_c - p[:, 128:]
                a_cur[h] = a * al
        for h in heads:
            a_full = jnp.broadcast_to(a_cur[h], (16, 128))
            a_hi = a_full.astype(BF16).astype(F32)
            send[h, 0:128, :] = b_cur[h].T.astype(BF16)
            send[h, 128:256, :] = s_cur[h].T.astype(BF16)
            send[h, 256:272, :] = jnp.where(row16 < 8, a_hi, a_full - a_hi).astype(BF16)

    def to_line(z):
        return remote(send.at[z], recv.at[zz], msend.at[z], mrecv.at[zz], at_z(z))

    def total_to(y):
        return remote(tsend, trecv.at[yy], tsems.at[y], tsems.at[LINE + yy], at_y(y))

    def give(z):
        return remote(step_out.at[z], entering.at[zz], osend.at[z], orecv.at[zz], at_z(z))

    for c in range(NC):
        for g in range(2):
            systems(c, g)
    invert()
    for c in range(NC):
        for g in range(2):
            unit(c, g)
    map_of(range(HEADS))

    for z in range(LINE):
        @pl.when(z > zz)
        def _(z=z):
            pl.semaphore_wait(ready.at[z], 1)

        @pl.when((z != zz) & (chip < LAST))
        def _(z=z):
            to_line(z).start()

    recv[zz] = send[zz]

    def local_part(c, carry):
        r = chunk_rows(c)
        cc_all = cum[c]
        a_all = ab[c]
        for h in range(HEADS):
            g = h // 2
            q = qs[r, g * 128 : (g + 1) * 128].astype(F32)
            o = dot(att[c * 4 + h], uw[c * 4 + h])
            qeff = jnp.exp(cc_all[:, h : h + 1]) * q - o[:, 128:]
            rr = dot(qeff.astype(BF16), sb[c * 4 + h])
            outloc[r, h * 128 : (h + 1) * 128] = o[:, :128] + rr[:, :128]
            reach[r, h * 128 : (h + 1) * 128] = (a_all[h : h + 1, :] * qeff + rr[:, 128:]).astype(BF16)
        return carry

    run(local_part)

    def arrived(z):
        @pl.when(z != zz)
        def _():
            remote(send.at[0], recv.at[z], msend.at[0], mrecv.at[z], partner).wait_recv()

    def factor(rows):
        v = rows.astype(F32)
        return v[0:1, :] + v[8:9, :]

    def split(a):
        full = jnp.broadcast_to(a, (16, 128))
        hi = full.astype(BF16).astype(F32)
        return jnp.where(row16 < 8, hi, full - hi).astype(BF16)

    def follow(x, a, m):
        bt = recv[m, 0:128, :]
        a_m = factor(recv[m, 256:272, :])
        after = jnp.concatenate([a * bt.astype(F32), recv[m, 128:256, :].astype(F32)], 0)
        return a_m * x + dot(x.astype(BF16), bt) + after, a * a_m

    for z in range(LINE - 1):
        arrived(z)
    x = recv[0, 0:256, :].astype(F32)
    a = factor(recv[0, 256:272, :])
    for z in range(1, LINE):
        pre_x[z - 1] = x
        pre_a[z - 1, 0:1, :] = a
        if z < LINE - 1:
            x, a = follow(x, a, z)

    @pl.when(yy < LINE - 1)
    def _():
        arrived(LINE - 1)
        t, t_a = follow(pre_x[LINE - 2], pre_a[LINE - 2, 0:1, :], LINE - 1)
        tsend[0:256, :] = t.astype(BF16)
        tsend[256:272, :] = split(t_a)
        for y in range(1, LINE):
            @pl.when(y > yy)
            def _(y=y):
                pl.semaphore_wait(ready.at[LINE + y], 1)
                total_to(y).start()

    for b in range(2):
        w_copies[4 + b].wait()
    gain = jnp.concatenate([norm_gain[...].reshape(1, 128)] * 2, 1)

    def gate_rows(t, carry):
        r = chunk_rows(t)
        h_rows = hid[chunk_rows(t), :]
        for b in range(2):
            zs[r, b * 256 : (b + 1) * 256] = silu(dot(h_rows, wbuf[4 + b])) * gain
        return carry

    run(gate_rows)

    st_copy.wait()
    st0[...] = st0[...].T
    for y in range(LINE - 1):
        @pl.when(y < yy)
        def _(y=y):
            remote(tsend, trecv.at[y], tsems.at[0], tsems.at[LINE + y], partner).wait_recv()
            s = st0[...]
            st0[...] = (
                factor(trecv[y, 256:272, :]) * s
                + dot(s.astype(BF16), trecv[y, 0:128, :])
                + trecv[y, 128:256, :].astype(F32)
            )

    s_line = st0[...]
    s_bf = s_line.astype(BF16)
    step_out[0] = s_bf
    for z in range(1, LINE):
        step_out[z] = (
            pre_a[z - 1, 0:1, :] * s_line + dot(s_bf, pre_x[z - 1, 0:128, :].astype(BF16)) + pre_x[z - 1, 128:256, :]
        ).astype(BF16)
    for z in range(LINE):
        @pl.when(z != zz)
        def _(z=z):
            give(z).start()

    entering[zz] = step_out[zz]
    for z in range(LINE):
        @pl.when(z != zz)
        def _(z=z):
            remote(step_out.at[0], entering.at[z], osend.at[0], orecv.at[z], partner).wait_recv()

    def finish(side, x, put):
        r = pl.ds(pl.multiple_of(side * OWN + x * 64, 64), 64)
        rz = pl.ds(pl.multiple_of(lax.select(side == core, 0, OWN) + x * 64, 64), 64)
        for h in range(HEADS):
            cols = slice(h * 128, (h + 1) * 128)
            o = outloc[r, cols] + dot_nt(reach[r, cols], entering[h])
            n = o * lax.rsqrt(jnp.mean(o * o, axis=-1, keepdims=True) + 1e-6) * zs[rz, cols]
            put(cols, n.astype(BF16))

    def to_partner(i, x):
        def put(cols, v):
            nsend[i, :, cols] = v

        finish(other, x, put)

    def keep(i, x):
        def put(cols, v):
            nfull[core, i, :, cols] = v

        finish(core, x, put)

    def block(i, n0, width):
        cols = slice(n0, n0 + width)
        return dot(nfull[0, i], wo[0:512, cols]) + dot(nfull[1, i], wo[512:1024, cols])

    def fill(dst, i, n0):
        for j in range(2):
            dst[:, j * 512 : (j + 1) * 512] = block(i, n0 + j * 512, 512).astype(BF16)

    n_first = remote(nsend.at[0], nfull.at[core, 0], nsem.at[0], nsem.at[2], partner)
    n_rest = remote(nsend.at[pl.ds(1, 3)], nfull.at[core, pl.ds(1, 3)], nsem.at[1], nsem.at[3], partner)
    to_partner(0, across)
    n_first.start()
    keep(0, across)
    for i, x in ((1, right), (2, left), (3, xx)):
        to_partner(i, x)
    n_rest.start()
    wo_copy.wait()
    n_first.wait_recv()

    relay_r = remote(rs_send.at[0], rs_relay.at[0], rsend.at[0], rrecv.at[0], at_x(right))
    relay_l = remote(rs_send.at[1], rs_relay.at[1], rsend.at[1], rrecv.at[1], at_x(left))
    direct_r = remote(rs_send.at[2], rs_arr.at[0], rsend.at[2], rrecv.at[2], at_x(right))
    direct_l = remote(rs_send.at[3], rs_arr.at[1], rsend.at[3], rrecv.at[3], at_x(left))
    sum_r = remote(rs_send.at[4], rs_arr.at[2], rsend.at[4], rrecv.at[4], at_x(right))
    sum_l = remote(rs_send.at[5], rs_arr.at[3], rsend.at[5], rrecv.at[5], at_x(left))
    fill(rs_send.at[0], 0, 0)
    relay_r.start()
    fill(rs_send.at[1], 0, 1024)
    relay_l.start()
    for i, x in ((1, right), (2, left), (3, xx)):
        keep(i, x)
    n_rest.wait_recv()
    fill(rs_send.at[2], 1, 1024)
    direct_r.start()
    fill(rs_send.at[3], 2, 0)
    direct_l.start()
    for j in range(2):
        rs_hold[0, :, j * 512 : (j + 1) * 512] = block(1, j * 512, 512)
    for j in range(2):
        rs_hold[1, :, j * 512 : (j + 1) * 512] = block(2, 1024 + j * 512, 512)
    relay_r.wait_recv()
    rs_send[4] = (rs_hold[0] + rs_relay[0].astype(F32)).astype(BF16)
    sum_r.start()
    relay_l.wait_recv()
    rs_send[5] = (rs_hold[1] + rs_relay[1].astype(F32)).astype(BF16)
    sum_l.start()
    for j in range(4):
        rs_own[:, j * 512 : (j + 1) * 512] = block(3, j * 512, 512)
    direct_r.wait_recv()
    direct_l.wait_recv()
    sum_r.wait_recv()
    sum_l.wait_recv()
    out[:, 0:1024] = (rs_own[:, 0:1024] + rs_arr[1].astype(F32) + rs_arr[2].astype(F32)).astype(BF16)
    out[:, 1024:2048] = (rs_own[:, 1024:2048] + rs_arr[0].astype(F32) + rs_arr[3].astype(F32)).astype(BF16)

    for cp in swaps:
        cp.wait_send()

    @pl.when(sends_halo)
    def _():
        halo0.wait_send()
        halo1.wait_send()

    for n in range(LINE):
        @pl.when((n != zz) & (chip < LAST))
        def _(n=n):
            to_line(n).wait_send()

        @pl.when(n > yy)
        def _(n=n):
            total_to(n).wait_send()

        @pl.when(n != zz)
        def _(n=n):
            give(n).wait_send()

    n_first.wait_send()
    n_rest.wait_send()
    for cp in (relay_r, relay_l, direct_r, direct_l, sum_r, sum_l):
        cp.wait_send()


def on_device(*args):
    any_space = pl.BlockSpec(memory_space=pl.ANY)
    vmem = pl.BlockSpec(memory_space=pltpu.VMEM)
    smem = pl.BlockSpec(memory_space=pltpu.SMEM)
    dma = pltpu.SemaphoreType.DMA
    return pl.pallas_call(
        kernel,
        out_shape=jax.ShapeDtypeStruct((64, DM), BF16),
        in_specs=[any_space] * 5 + [vmem] * 5 + [smem] * 3 + [vmem] + [any_space] * 2,
        out_specs=vmem,
        scratch_shapes=[
            pltpu.VMEM((HALO + ROWS, DM), BF16),
            pltpu.VMEM((6, DM, 256), BF16),
            pltpu.VMEM((1024, DM), BF16),
            pltpu.VMEM((128, 128), F32),
            *[pltpu.VMEM((HALO + ROWS, 256), F32)] * 4,
            pltpu.VMEM((ROWS, 256), BF16),
            pltpu.VMEM((ROWS, 256), BF16),
            pltpu.VMEM((ROWS, 512), F32),
            pltpu.VMEM((ROWS, 512), F32),
            pltpu.VMEM((NC, CH, 128), F32),
            pltpu.VMEM((NC, 8, CH), F32),
            pltpu.VMEM((8, CH, 256), BF16),
            pltpu.VMEM((8, CH, 256), BF16),
            pltpu.VMEM((16, CH, CH), BF16),
            pltpu.VMEM((16, CH, 256), BF16),
            pltpu.VMEM((16, 128, 256), F32),
            pltpu.VMEM((16, 128, 256), BF16),
            pltpu.VMEM((NC, 8, 128), F32),
            pltpu.VMEM((ROWS, 512), BF16),
            pltpu.VMEM((ROWS, 512), F32),
            pltpu.VMEM((HEADS, MSG, 128), BF16),
            pltpu.VMEM((LINE, MSG, 128), BF16),
            pltpu.VMEM((MSG, 128), BF16),
            pltpu.VMEM((LINE, MSG, 128), BF16),
            pltpu.VMEM((LINE - 1, 256, 128), F32),
            pltpu.VMEM((LINE - 1, 8, 128), F32),
            pltpu.VMEM((LINE, 128, 128), BF16),
            pltpu.VMEM((HEADS, 128, 128), BF16),
            pltpu.VMEM((4, 64, 512), BF16),
            pltpu.VMEM((2, 4, 64, 512), BF16),
            pltpu.VMEM((6, 64, 1024), BF16),
            pltpu.VMEM((2, 64, 1024), BF16),
            pltpu.VMEM((4, 64, 1024), BF16),
            pltpu.VMEM((64, DM), F32),
            pltpu.VMEM((2, 64, 1024), F32),
            dma((5,)),
            dma((6,)),
            dma((8,)),
            dma((3,)),
            dma((HEADS,)),
            dma((LINE,)),
            dma((2 * LINE,)),
            dma((LINE,)),
            dma((LINE,)),
            dma((4,)),
            dma((6,)),
            dma((6,)),
            pltpu.SemaphoreType.REGULAR((2 * LINE,)),
        ],
        compiler_params=pltpu.CompilerParams(
            collective_id=0, has_side_effects=True, vmem_limit_bytes=56 * 1024 * 1024
        ),
    )(*args[:5], args[5].T, args[6].T, *args[7:])


def solution(mesh):
    placed = (
        P("seq", None),
        P(None, "head"),
        P(None, "head"),
        P(None, "head"),
        P(None, "head"),
        P(None, "head"),
        P(None, "head"),
        P(None, "head"),
        P(None, "head"),
        P(None, "head"),
        P("head"),
        P("head"),
        P("head"),
        P(),
        P("head", None),
        P("head", None, None),
    )
    return jax.shard_map(
        on_device, mesh=mesh, in_specs=placed, out_specs=P(("seq", "head"), None), check_vma=False
    )
```

```python
import jax
import jax.numpy as jnp
from jax import lax
from jax.experimental import pallas as pl
from jax.experimental.pallas import tpu as pltpu
from jax.sharding import PartitionSpec as P

MESH = pl.DeviceIdType.MESH
F32 = jnp.float32
BF16 = jnp.bfloat16
HALO = 16
OWN = 256
ROWS = 512
DM = 2048
CH = 128
NC = ROWS // CH
HEADS = 4
CHIPS = 16
MSG = 272
LAST = CHIPS - 1
LINE = 4


def dot(a, b):
    return jnp.dot(a, b, preferred_element_type=F32)


def dot_nt(a, b):
    return lax.dot_general(a, b, (((1,), (1,)), ((), ())), preferred_element_type=F32)


def silu(u):
    return u * jax.nn.sigmoid(u)


def kernel(
    hidden, w_query, w_key, w_value, w_gate_z, w_decay, w_beta, conv_query, conv_key, conv_value,
    decay_log, decay_bias, beta_bias, norm_gain, w_out, state_in,
    out,
    hid, wbuf, wo, st0, raw0, raw1, raw2, raw3, qs, ks, vs, zs, cum, cumt, low, tri, att, uw, ee, sb, ab,
    reach, outloc, send, recv, tsend, trecv, pre_x, pre_a, step_out, entering, nsend, nfull, rs_send, rs_relay, rs_arr, rs_own, rs_hold,
    lsem, wsem, xsem, hsem, msend, mrecv, tsems, osend, orecv, nsem, rsend, rrecv, ready,
):
    seq = lax.axis_index("seq")
    xx = lax.axis_index("head")
    chip = seq // 2
    core = seq % 2
    other = 1 - core
    partner = (chip * 2 + other, xx)
    nxt = lax.rem(chip + 1, CHIPS)
    prv = lax.rem(chip + CHIPS - 1, CHIPS)
    right = lax.rem(xx + 1, 4)
    left = lax.rem(xx + 3, 4)
    across = lax.rem(xx + 2, 4)

    def at_x(x):
        return (seq, x)

    def local(src, dst, sem):
        return pltpu.make_async_copy(src, dst, sem)

    def remote(src, dst, s_sem, r_sem, device):
        return pltpu.make_async_remote_copy(
            src_ref=src, dst_ref=dst, send_sem=s_sem, recv_sem=r_sem, device_id=device, device_id_type=MESH
        )

    col256 = pl.ds(pl.multiple_of(core * 256, 256), 256)
    zz = lax.rem(chip, LINE)
    yy = chip // LINE

    def at_z(z):
        return ((yy * LINE + z) * 2 + core, xx)

    def at_y(y):
        return ((y * LINE + zz) * 2 + core, xx)

    def chunk_rows(c):
        return pl.ds(c * CH, CH)

    def run(step):
        for c in range(NC):
            step(c, 0)

    own_copy = local(hidden, hid.at[pl.ds(0, OWN), :], lsem.at[0])
    own_copy.start()
    w_copies = [
        local(w_query.at[:, col256], wbuf.at[0], wsem.at[0]),
        local(w_key.at[:, col256], wbuf.at[1], wsem.at[1]),
    ]
    for i in range(2):
        cols = pl.ds(pl.multiple_of(core * 512 + i * 256, 256), 256)
        w_copies.append(local(w_value.at[:, cols], wbuf.at[2 + i], wsem.at[2 + i]))
    for i in range(2):
        cols = pl.ds(pl.multiple_of(core * 512 + i * 256, 256), 256)
        w_copies.append(local(w_gate_z.at[:, cols], wbuf.at[4 + i], wsem.at[4 + i]))
    for cp in w_copies[:4]:
        cp.start()
    st_copy = local(state_in.at[core * HEADS + zz], st0, lsem.at[3])
    wo_copy = local(w_out, wo, lsem.at[4])

    barrier = pltpu.get_barrier_semaphore()

    def greet(device):
        pl.semaphore_signal(barrier, inc=1, device_id=device, device_id_type=MESH)

    greet(partner)
    greet(at_x(right))
    greet(at_x(left))

    @pl.when(chip > 0)
    def _():
        greet((prv * 2 + 1, xx))

    for n in range(1, LINE):
        @pl.when(n > zz)
        def _(n=n):
            greet(at_z(n))

        @pl.when(n > yy)
        def _(n=n):
            greet(at_y(n))

    sends_halo = (core == 1) & (chip < LAST)
    pl.semaphore_wait(barrier, 3 + zz + yy + lax.select(sends_halo, 2, 0))

    swaps = [
        remote(
            hidden.at[pl.ds(i * 64, 64), :], hid.at[pl.ds(OWN + i * 64, 64), :], xsem.at[i], xsem.at[4 + i], partner
        )
        for i in range(4)
    ]
    for cp in swaps:
        cp.start()
    tail = hidden.at[pl.ds(OWN - HALO, HALO), :]
    halo_at = hid.at[pl.ds(ROWS, HALO), :]
    halo0 = remote(tail, halo_at, hsem.at[0], hsem.at[2], (nxt * 2, xx))
    halo1 = remote(tail, halo_at, hsem.at[1], hsem.at[2], (nxt * 2 + 1, xx))

    @pl.when(sends_halo)
    def _():
        halo0.start()
        halo1.start()

    for n in range(LINE - 1):
        @pl.when(n < zz)
        def _(n=n):
            pl.semaphore_signal(ready.at[zz], inc=1, device_id=at_z(n), device_id_type=MESH)

        @pl.when(n < yy)
        def _(n=n):
            pl.semaphore_signal(ready.at[LINE + yy], inc=1, device_id=at_y(n), device_id_type=MESH)

    raws = (raw0, raw1, raw2, raw3)
    rows_own = pl.ds(pl.multiple_of(HALO + core * OWN, 16), OWN)
    rows_other = pl.ds(pl.multiple_of(HALO + other * OWN, 16), OWN)
    own_copy.wait()
    for b in range(4):
        w_copies[b].wait()
        raws[b][rows_own, :] = dot(hid[0:OWN, :], wbuf[b]).astype(BF16).astype(F32)
    for cp in w_copies[4:]:
        cp.start()
    st_copy.start()
    wo_copy.start()
    for cp in swaps:
        cp.wait_recv()

    @pl.when(chip > 0)
    def _():
        halo0.wait_recv()

    @pl.when(chip == 0)
    def _():
        hid[ROWS : ROWS + HALO, :] = jnp.zeros((HALO, DM), BF16)

    taps_of = (
        lambda: conv_query[:, col256].astype(F32),
        lambda: conv_key[:, col256].astype(F32),
        lambda: conv_value[:, pl.ds(pl.multiple_of(core * 512, 256), 256)].astype(F32),
        lambda: conv_value[:, pl.ds(pl.multiple_of(core * 512 + 256, 256), 256)].astype(F32),
    )
    for b in range(4):
        raw = raws[b]
        rest = dot(hid[OWN : ROWS + HALO, :], wbuf[b]).astype(BF16).astype(F32)
        raw[rows_other, :] = rest[:OWN]
        raw[0:HALO, :] = rest[OWN:]
        taps = taps_of[b]()
        for t in range(NC):
            pre = jnp.zeros((CH, 256), F32)
            for i in range(4):
                pre = pre + taps[i : i + 1, :] * raw[pl.ds(HALO - 3 + i + t * CH, CH), :]
            act = silu(pre)
            r = pl.ds(t * CH, CH)
            if b < 2:
                for g in range(2):
                    a = act[:, g * 128 : (g + 1) * 128]
                    n = a * lax.rsqrt(jnp.sum(a * a, axis=-1, keepdims=True) + 1e-6)
                    if b == 0:
                        qs[r, g * 128 : (g + 1) * 128] = (n * 128 ** (-0.5)).astype(BF16)
                    else:
                        ks[r, g * 128 : (g + 1) * 128] = n.astype(BF16)
            else:
                vs[r, (b - 2) * 256 : (b - 1) * 256] = act

    head_row = lax.broadcasted_iota(jnp.int32, (HEADS, 1), 0)

    def column_of(ref):
        v = jnp.zeros((HEADS, 1), F32)
        for h in range(HEADS):
            v = jnp.where(head_row == h, ref[core * HEADS + h], v)
        return v

    rate = -jnp.exp(column_of(decay_log))
    ti = lax.broadcasted_iota(jnp.int32, (CH, CH), 0)
    tj = lax.broadcasted_iota(jnp.int32, (CH, CH), 1)
    incl = ti >= tj
    ones_up = jnp.where(ti <= tj, 1.0, 0.0).astype(F32)
    w_gates = jnp.concatenate([w_decay[...].astype(F32), w_beta[...].astype(F32)], 0).astype(BF16)
    lg = dot_nt(w_gates, hid[0:ROWS, :])
    logits = jnp.concatenate(
        [jnp.where(core == 0, lg[:, :OWN], lg[:, OWN:]), jnp.where(core == 0, lg[:, OWN:], lg[:, :OWN])], 1
    )
    u = jnp.where(core == 0, logits[0:4], logits[4:8]) + column_of(decay_bias)
    glog = rate * (jnp.maximum(u, 0.0) + jnp.log1p(jnp.exp(-jnp.abs(u))))
    strength = jax.nn.sigmoid(jnp.where(core == 0, logits[8:12], logits[12:16]) + column_of(beta_bias))
    pad4 = jnp.zeros((4, CH), F32)
    for t in range(NC):
        cols = slice(t * CH, (t + 1) * CH)
        g8 = jnp.concatenate([glog[:, cols], pad4], 0)
        cr8 = jnp.dot(g8, ones_up, precision=lax.Precision.HIGHEST, preferred_element_type=F32)
        cumt[t] = cr8
        stacked = jnp.concatenate([cr8, strength[:, cols], jnp.zeros((CH - 12, CH), F32)], 0)
        cum[t] = stacked.T

    z128 = jnp.zeros((CH, CH), BF16)

    def pair_diag(m):
        return jnp.concatenate(
            [jnp.concatenate([m[:, :128], z128], 1), jnp.concatenate([z128, m[:, 128:]], 1)], 0
        )

    pi = lax.broadcasted_iota(jnp.int32, (CH, 256), 0)
    pj = lax.broadcasted_iota(jnp.int32, (CH, 256), 1) % 128
    pxor = pi ^ pj
    row16 = lax.broadcasted_iota(jnp.int32, (16, 128), 0)

    def systems(c, g):
        r = chunk_rows(c)
        cc_all = cum[c]
        cr_all = cumt[c]
        k = ks[r, g * 128 : (g + 1) * 128]
        q = qs[r, g * 128 : (g + 1) * 128]
        both = dot_nt(jnp.concatenate([k, q], 0), k)
        kk, qk = both[:CH], both[CH:]
        for e in range(2):
            h = 2 * g + e
            diff = cc_all[:, h : h + 1] - cr_all[h : h + 1, :]
            ratio = jnp.exp(jnp.where(incl, diff, -1e30))
            lo = jnp.where(ti > tj, cc_all[:, 8 + h : 9 + h] * ratio * kk, 0.0)
            low[c * 2 + g, :, e * 128 : (e + 1) * 128] = lo.astype(BF16)
            att[c * 4 + h] = (ratio * qk).astype(BF16)
            tri[c * 2 + g, :, e * 128 : (e + 1) * 128] = jnp.where(
                ti == tj, 1.0, jnp.where((ti ^ tj) == 1, -lo, 0.0)
            ).astype(BF16)

    def invert():
        pairs = range(2 * NC)

        def double(level, size):
            mask = (pxor >= size) & (pxor < 2 * size)
            prods = []
            for p in pairs:
                lm = jnp.where(mask, low[p].astype(F32), 0.0).astype(BF16)
                prods.append(dot(tri[p], pair_diag(lm)).astype(BF16))
            for p, prod in zip(pairs, prods):
                t_old = tri[p]
                y = dot(prod, pair_diag(t_old))
                tri[p] = (t_old.astype(F32) - y).astype(BF16)
            return size * 2

        lax.fori_loop(0, 6, double, jnp.int32(2))

    def unit(c, g):
        r = chunk_rows(c)
        cc_all = cum[c]
        cr_all = cumt[c]
        k = ks[r, g * 128 : (g + 1) * 128].astype(F32)
        kt = k.T
        for e in range(2):
            h = 2 * g + e
            be = cc_all[:, 8 + h : 9 + h]
            cc = cc_all[:, h : h + 1]
            cr = cr_all[h : h + 1, :]
            tail_w = jnp.exp(cr[:, 127:128] - cr)
            rhs = jnp.concatenate([be * vs[r, h * 128 : (h + 1) * 128], (be * jnp.exp(cc)) * k], 1)
            u = dot(tri[c * 2 + g, :, e * 128 : (e + 1) * 128], rhs.astype(BF16)).astype(BF16)
            uw[c * 4 + h] = u
            ee[c * 4 + h] = dot((kt * tail_w).astype(BF16), u)

    def map_of(heads):
        s_cur, b_cur, a_cur = {}, {}, {}
        for h in heads:
            e0 = ee[h]
            s_cur[h] = e0[:, :128]
            b_cur[h] = -e0[:, 128:]
            a_cur[h] = jnp.exp(cumt[0, h : h + 1, 127:128])
            sb[h] = jnp.zeros((128, 256), BF16)
            ab[0, h : h + 1, :] = jnp.ones((1, 128), F32)
        for c in range(1, NC):
            for h in heads:
                s, bm, a = s_cur[h], b_cur[h], a_cur[h]
                packed = jnp.concatenate([s, bm], 1).astype(BF16)
                sb[c * 4 + h] = packed
                ab[c, h : h + 1, :] = jnp.broadcast_to(a, (1, 128))
                e_c = ee[c * 4 + h]
                m_c = e_c[:, 128:]
                p = dot(m_c.astype(BF16), packed)
                al = jnp.exp(cumt[c, h : h + 1, 127:128])
                s_cur[h] = al * s - p[:, :128] + e_c[:, :128]
                b_cur[h] = al * bm - a * m_c - p[:, 128:]
                a_cur[h] = a * al
        for h in heads:
            a_full = jnp.broadcast_to(a_cur[h], (16, 128))
            a_hi = a_full.astype(BF16).astype(F32)
            send[h, 0:128, :] = b_cur[h].T.astype(BF16)
            send[h, 128:256, :] = s_cur[h].T.astype(BF16)
            send[h, 256:272, :] = jnp.where(row16 < 8, a_hi, a_full - a_hi).astype(BF16)

    def to_line(z):
        return remote(send.at[z], recv.at[zz], msend.at[z], mrecv.at[zz], at_z(z))

    def total_to(y):
        return remote(tsend, trecv.at[yy], tsems.at[y], tsems.at[LINE + yy], at_y(y))

    half = pl.ds(128, 128)

    def state_to(y):
        return remote(tsend.at[half], trecv.at[0, half], tsems.at[y], tsems.at[LINE], at_y(y))

    def give(z):
        return remote(step_out.at[z], entering.at[zz], osend.at[z], orecv.at[zz], at_z(z))

    for c in range(NC):
        for g in range(2):
            systems(c, g)
    invert()
    for c in range(NC):
        for g in range(2):
            unit(c, g)
    map_of(range(HEADS))

    for z in range(1, LINE):
        @pl.when(z > zz)
        def _(z=z):
            pl.semaphore_wait(ready.at[z], 1)

    @pl.when(chip < LAST)
    def _():
        for k in (2, 3, 1):
            to_line(lax.rem(zz + k, LINE)).start()

    recv[zz] = send[zz]

    def local_part(c, carry):
        r = chunk_rows(c)
        cc_all = cum[c]
        a_all = ab[c]
        for h in range(HEADS):
            g = h // 2
            q = qs[r, g * 128 : (g + 1) * 128].astype(F32)
            o = dot(att[c * 4 + h], uw[c * 4 + h])
            qeff = jnp.exp(cc_all[:, h : h + 1]) * q - o[:, 128:]
            rr = dot(qeff.astype(BF16), sb[c * 4 + h])
            outloc[r, h * 128 : (h + 1) * 128] = o[:, :128] + rr[:, :128]
            reach[r, h * 128 : (h + 1) * 128] = (a_all[h : h + 1, :] * qeff + rr[:, 128:]).astype(BF16)
        return carry

    run(local_part)

    def arrived(z):
        @pl.when(z != zz)
        def _():
            remote(send.at[0], recv.at[z], msend.at[0], mrecv.at[z], partner).wait_recv()

    def factor(rows):
        v = rows.astype(F32)
        return v[0:1, :] + v[8:9, :]

    def split(a):
        full = jnp.broadcast_to(a, (16, 128))
        hi = full.astype(BF16).astype(F32)
        return jnp.where(row16 < 8, hi, full - hi).astype(BF16)

    def follow(x, a, m):
        bt = recv[m, 0:128, :]
        a_m = factor(recv[m, 256:272, :])
        after = jnp.concatenate([a * bt.astype(F32), recv[m, 128:256, :].astype(F32)], 0)
        return a_m * x + dot(x.astype(BF16), bt) + after, a * a_m

    st_copy.wait()
    st0[...] = st0[...].T
    for z in range(LINE - 1):
        arrived(z)
    x = recv[0, 0:256, :].astype(F32)
    a = factor(recv[0, 256:272, :])
    for z in range(1, LINE):
        pre_x[z - 1] = x
        pre_a[z - 1, 0:1, :] = a
        if z < LINE - 1:
            x, a = follow(x, a, z)

    @pl.when(yy < LINE - 1)
    def _():
        arrived(LINE - 1)
        t, t_a = follow(pre_x[LINE - 2], pre_a[LINE - 2, 0:1, :], LINE - 1)
        for y in range(1, LINE):
            @pl.when(y > yy)
            def _(y=y):
                pl.semaphore_wait(ready.at[LINE + y], 1)

        @pl.when(yy == 0)
        def _():
            s = st0[...]
            tsend[128:256, :] = (t_a * s + dot(s.astype(BF16), t[0:128].astype(BF16)) + t[128:256]).astype(BF16)
            for y in range(1, LINE):
                state_to(y).start()

        @pl.when(yy > 0)
        def _():
            tsend[0:256, :] = t.astype(BF16)
            tsend[256:272, :] = split(t_a)
            for y in range(2, LINE):
                @pl.when(y > yy)
                def _(y=y):
                    total_to(y).start()

    for b in range(2):
        w_copies[4 + b].wait()
    gain = jnp.concatenate([norm_gain[...].reshape(1, 128)] * 2, 1)

    def gate_rows(t, carry):
        r = chunk_rows(t)
        h_rows = hid[chunk_rows(t), :]
        for b in range(2):
            zs[r, b * 256 : (b + 1) * 256] = silu(dot(h_rows, wbuf[4 + b])) * gain
        return carry

    run(gate_rows)

    @pl.when(yy > 0)
    def _():
        remote(tsend.at[half], trecv.at[0, half], tsems.at[0], tsems.at[LINE], partner).wait_recv()
        st0[...] = trecv[0, 128:256, :].astype(F32)

    for y in range(1, LINE - 1):
        @pl.when(y < yy)
        def _(y=y):
            remote(tsend, trecv.at[y], tsems.at[0], tsems.at[LINE + y], partner).wait_recv()
            s = st0[...]
            st0[...] = (
                factor(trecv[y, 256:272, :]) * s
                + dot(s.astype(BF16), trecv[y, 0:128, :])
                + trecv[y, 128:256, :].astype(F32)
            )

    s_line = st0[...]
    s_bf = s_line.astype(BF16)
    step_out[0] = s_bf
    for z in range(1, LINE):
        step_out[z] = (
            pre_a[z - 1, 0:1, :] * s_line + dot(s_bf, pre_x[z - 1, 0:128, :].astype(BF16)) + pre_x[z - 1, 128:256, :]
        ).astype(BF16)
    for k in (2, 3, 1):
        give(lax.rem(zz + k, LINE)).start()
    entering[zz] = step_out[zz]
    for z in range(LINE):
        @pl.when(z != zz)
        def _(z=z):
            remote(step_out.at[0], entering.at[z], osend.at[0], orecv.at[z], partner).wait_recv()

    def finish(side, x, put):
        r = pl.ds(pl.multiple_of(side * OWN + x * 64, 64), 64)
        rz = pl.ds(pl.multiple_of(lax.select(side == core, 0, OWN) + x * 64, 64), 64)
        for h in range(HEADS):
            cols = slice(h * 128, (h + 1) * 128)
            o = outloc[r, cols] + dot_nt(reach[r, cols], entering[h])
            n = o * lax.rsqrt(jnp.mean(o * o, axis=-1, keepdims=True) + 1e-6) * zs[rz, cols]
            put(cols, n.astype(BF16))

    def to_partner(i, x):
        def put(cols, v):
            nsend[i, :, cols] = v

        finish(other, x, put)

    def keep(i, x):
        def put(cols, v):
            nfull[core, i, :, cols] = v

        finish(core, x, put)

    def block(i, n0, width):
        cols = slice(n0, n0 + width)
        return dot(nfull[0, i], wo[0:512, cols]) + dot(nfull[1, i], wo[512:1024, cols])

    def fill(dst, i, n0):
        for j in range(2):
            dst[:, j * 512 : (j + 1) * 512] = block(i, n0 + j * 512, 512).astype(BF16)

    n_first = remote(nsend.at[0], nfull.at[core, 0], nsem.at[0], nsem.at[2], partner)
    n_rest = remote(nsend.at[pl.ds(1, 3)], nfull.at[core, pl.ds(1, 3)], nsem.at[1], nsem.at[3], partner)
    to_partner(0, across)
    n_first.start()
    keep(0, across)
    to_partner(1, right)
    wo_copy.wait()
    n_first.wait_recv()

    relay_r = remote(rs_send.at[0], rs_relay.at[0], rsend.at[0], rrecv.at[0], at_x(right))
    relay_l = remote(rs_send.at[1], rs_relay.at[1], rsend.at[1], rrecv.at[1], at_x(left))
    direct_r = remote(rs_send.at[2], rs_arr.at[0], rsend.at[2], rrecv.at[2], at_x(right))
    direct_l = remote(rs_send.at[3], rs_arr.at[1], rsend.at[3], rrecv.at[3], at_x(left))
    sum_r = remote(rs_send.at[4], rs_arr.at[2], rsend.at[4], rrecv.at[4], at_x(right))
    sum_l = remote(rs_send.at[5], rs_arr.at[3], rsend.at[5], rrecv.at[5], at_x(left))
    fill(rs_send.at[0], 0, 0)
    relay_r.start()
    fill(rs_send.at[1], 0, 1024)
    relay_l.start()
    to_partner(2, left)
    to_partner(3, xx)
    n_rest.start()
    for i, x in ((1, right), (2, left), (3, xx)):
        keep(i, x)
    n_rest.wait_recv()
    fill(rs_send.at[2], 1, 1024)
    direct_r.start()
    fill(rs_send.at[3], 2, 0)
    direct_l.start()
    for j in range(2):
        rs_hold[0, :, j * 512 : (j + 1) * 512] = block(1, j * 512, 512)
    for j in range(2):
        rs_hold[1, :, j * 512 : (j + 1) * 512] = block(2, 1024 + j * 512, 512)
    relay_r.wait_recv()
    rs_send[4] = (rs_hold[0] + rs_relay[0].astype(F32)).astype(BF16)
    sum_r.start()
    relay_l.wait_recv()
    rs_send[5] = (rs_hold[1] + rs_relay[1].astype(F32)).astype(BF16)
    sum_l.start()
    for j in range(4):
        rs_own[:, j * 512 : (j + 1) * 512] = block(3, j * 512, 512)
    direct_r.wait_recv()
    direct_l.wait_recv()
    rs_own[:, 0:1024] += rs_arr[1].astype(F32)
    rs_own[:, 1024:2048] += rs_arr[0].astype(F32)
    sum_r.wait_recv()
    out[:, 0:1024] = (rs_own[:, 0:1024] + rs_arr[2].astype(F32)).astype(BF16)
    sum_l.wait_recv()
    out[:, 1024:2048] = (rs_own[:, 1024:2048] + rs_arr[3].astype(F32)).astype(BF16)

    for cp in swaps:
        cp.wait_send()

    @pl.when(sends_halo)
    def _():
        halo0.wait_send()
        halo1.wait_send()

    for n in range(LINE):
        @pl.when((n != zz) & (chip < LAST))
        def _(n=n):
            to_line(n).wait_send()

        @pl.when((n > yy) & (yy > 0))
        def _(n=n):
            total_to(n).wait_send()

        if n > 0:
            @pl.when(yy == 0)
            def _(n=n):
                state_to(n).wait_send()

        @pl.when(n != zz)
        def _(n=n):
            give(n).wait_send()

    n_first.wait_send()
    n_rest.wait_send()
    for cp in (relay_r, relay_l, direct_r, direct_l, sum_r, sum_l):
        cp.wait_send()


def on_device(*args):
    any_space = pl.BlockSpec(memory_space=pl.ANY)
    vmem = pl.BlockSpec(memory_space=pltpu.VMEM)
    smem = pl.BlockSpec(memory_space=pltpu.SMEM)
    dma = pltpu.SemaphoreType.DMA
    return pl.pallas_call(
        kernel,
        out_shape=jax.ShapeDtypeStruct((64, DM), BF16),
        in_specs=[any_space] * 5 + [vmem] * 5 + [smem] * 3 + [vmem] + [any_space] * 2,
        out_specs=vmem,
        scratch_shapes=[
            pltpu.VMEM((HALO + ROWS, DM), BF16),
            pltpu.VMEM((6, DM, 256), BF16),
            pltpu.VMEM((1024, DM), BF16),
            pltpu.VMEM((128, 128), F32),
            *[pltpu.VMEM((HALO + ROWS, 256), F32)] * 4,
            pltpu.VMEM((ROWS, 256), BF16),
            pltpu.VMEM((ROWS, 256), BF16),
            pltpu.VMEM((ROWS, 512), F32),
            pltpu.VMEM((ROWS, 512), F32),
            pltpu.VMEM((NC, CH, 128), F32),
            pltpu.VMEM((NC, 8, CH), F32),
            pltpu.VMEM((8, CH, 256), BF16),
            pltpu.VMEM((8, CH, 256), BF16),
            pltpu.VMEM((16, CH, CH), BF16),
            pltpu.VMEM((16, CH, 256), BF16),
            pltpu.VMEM((16, 128, 256), F32),
            pltpu.VMEM((16, 128, 256), BF16),
            pltpu.VMEM((NC, 8, 128), F32),
            pltpu.VMEM((ROWS, 512), BF16),
            pltpu.VMEM((ROWS, 512), F32),
            pltpu.VMEM((HEADS, MSG, 128), BF16),
            pltpu.VMEM((LINE, MSG, 128), BF16),
            pltpu.VMEM((MSG, 128), BF16),
            pltpu.VMEM((LINE, MSG, 128), BF16),
            pltpu.VMEM((LINE - 1, 256, 128), F32),
            pltpu.VMEM((LINE - 1, 8, 128), F32),
            pltpu.VMEM((LINE, 128, 128), BF16),
            pltpu.VMEM((HEADS, 128, 128), BF16),
            pltpu.VMEM((4, 64, 512), BF16),
            pltpu.VMEM((2, 4, 64, 512), BF16),
            pltpu.VMEM((6, 64, 1024), BF16),
            pltpu.VMEM((2, 64, 1024), BF16),
            pltpu.VMEM((4, 64, 1024), BF16),
            pltpu.VMEM((64, DM), F32),
            pltpu.VMEM((2, 64, 1024), F32),
            dma((5,)),
            dma((6,)),
            dma((8,)),
            dma((3,)),
            dma((HEADS,)),
            dma((LINE,)),
            dma((2 * LINE,)),
            dma((LINE,)),
            dma((LINE,)),
            dma((4,)),
            dma((6,)),
            dma((6,)),
            pltpu.SemaphoreType.REGULAR((2 * LINE,)),
        ],
        compiler_params=pltpu.CompilerParams(
            collective_id=0, has_side_effects=True, vmem_limit_bytes=56 * 1024 * 1024
        ),
    )(*args[:5], args[5].T, args[6].T, *args[7:])


def solution(mesh):
    placed = (
        P("seq", None),
        P(None, "head"),
        P(None, "head"),
        P(None, "head"),
        P(None, "head"),
        P(None, "head"),
        P(None, "head"),
        P(None, "head"),
        P(None, "head"),
        P(None, "head"),
        P("head"),
        P("head"),
        P("head"),
        P(),
        P("head", None),
        P("head", None, None),
    )
    return jax.shard_map(
        on_device, mesh=mesh, in_specs=placed, out_specs=P(("seq", "head"), None), check_vma=False
    )
```

```python
import jax
import jax.numpy as jnp
from jax import lax
from jax.experimental import pallas as pl
from jax.experimental.pallas import tpu as pltpu
from jax.sharding import PartitionSpec as P

MESH = pl.DeviceIdType.MESH
F32 = jnp.float32
BF16 = jnp.bfloat16
HALO = 16
OWN = 256
ROWS = 512
DM = 2048
CH = 128
NC = ROWS // CH
HEADS = 4
CHIPS = 16
MSG = 272
LAST = CHIPS - 1
LINE = 4


def dot(a, b):
    return jnp.dot(a, b, preferred_element_type=F32)


def dot_nt(a, b):
    return lax.dot_general(a, b, (((1,), (1,)), ((), ())), preferred_element_type=F32)


def silu(u):
    return u * jax.nn.sigmoid(u)


def kernel(
    hidden, w_query, w_key, w_value, w_gate_z, w_decay, w_beta, conv_query, conv_key, conv_value,
    decay_log, decay_bias, beta_bias, norm_gain, w_out, state_in,
    out,
    hid, wbuf, wo, st0, raw0, raw1, raw2, raw3, qs, ks, vs, zs, cum, cumt, low, tri, att, uw, ee, sb, ab,
    reach, outloc, send, recv, tsend, trecv, pre_x, pre_a, step_out, entering, nsend, nfull, rs_send, rs_relay, rs_arr, rs_own, rs_hold,
    lsem, wsem, xsem, hsem, msend, mrecv, tsems, osend, orecv, nsem, rsend, rrecv, ready,
):
    seq = lax.axis_index("seq")
    xx = lax.axis_index("head")
    chip = seq // 2
    core = seq % 2
    other = 1 - core
    partner = (chip * 2 + other, xx)
    nxt = lax.rem(chip + 1, CHIPS)
    prv = lax.rem(chip + CHIPS - 1, CHIPS)
    right = lax.rem(xx + 1, 4)
    left = lax.rem(xx + 3, 4)
    across = lax.rem(xx + 2, 4)

    def at_x(x):
        return (seq, x)

    def local(src, dst, sem):
        return pltpu.make_async_copy(src, dst, sem)

    def remote(src, dst, s_sem, r_sem, device):
        return pltpu.make_async_remote_copy(
            src_ref=src, dst_ref=dst, send_sem=s_sem, recv_sem=r_sem, device_id=device, device_id_type=MESH
        )

    col256 = pl.ds(pl.multiple_of(core * 256, 256), 256)
    zz = lax.rem(chip, LINE)
    yy = chip // LINE

    def at_z(z):
        return ((yy * LINE + z) * 2 + core, xx)

    def at_y(y):
        return ((y * LINE + zz) * 2 + core, xx)

    def chunk_rows(c):
        return pl.ds(c * CH, CH)

    def run(step):
        for c in range(NC):
            step(c, 0)

    own_copy = local(hidden, hid.at[pl.ds(0, OWN), :], lsem.at[0])
    own_copy.start()
    w_copies = [
        local(w_query.at[:, col256], wbuf.at[0], wsem.at[0]),
        local(w_key.at[:, col256], wbuf.at[1], wsem.at[1]),
    ]
    for i in range(2):
        cols = pl.ds(pl.multiple_of(core * 512 + i * 256, 256), 256)
        w_copies.append(local(w_value.at[:, cols], wbuf.at[2 + i], wsem.at[2 + i]))
    for i in range(2):
        cols = pl.ds(pl.multiple_of(core * 512 + i * 256, 256), 256)
        w_copies.append(local(w_gate_z.at[:, cols], wbuf.at[4 + i], wsem.at[4 + i]))
    for cp in w_copies[:4]:
        cp.start()
    st_copy = local(state_in.at[core * HEADS + zz], st0, lsem.at[3])
    wo_copy = local(w_out, wo, lsem.at[4])

    barrier = pltpu.get_barrier_semaphore()

    def greet(device):
        pl.semaphore_signal(barrier, inc=1, device_id=device, device_id_type=MESH)

    greet(partner)
    greet(at_x(right))
    greet(at_x(left))

    @pl.when(chip > 0)
    def _():
        greet((prv * 2 + 1, xx))

    for n in range(1, LINE):
        @pl.when(n > zz)
        def _(n=n):
            greet(at_z(n))

        @pl.when(n > yy)
        def _(n=n):
            greet(at_y(n))

    sends_halo = (core == 1) & (chip < LAST)
    pl.semaphore_wait(barrier, 3 + zz + yy + lax.select(sends_halo, 2, 0))

    swaps = [
        remote(
            hidden.at[pl.ds(i * 64, 64), :], hid.at[pl.ds(OWN + i * 64, 64), :], xsem.at[i], xsem.at[4 + i], partner
        )
        for i in range(4)
    ]
    for cp in swaps:
        cp.start()
    tail = hidden.at[pl.ds(OWN - HALO, HALO), :]
    halo_at = hid.at[pl.ds(ROWS, HALO), :]
    halo0 = remote(tail, halo_at, hsem.at[0], hsem.at[2], (nxt * 2, xx))
    halo1 = remote(tail, halo_at, hsem.at[1], hsem.at[2], (nxt * 2 + 1, xx))

    @pl.when(sends_halo)
    def _():
        halo0.start()
        halo1.start()

    for n in range(LINE - 1):
        @pl.when(n < zz)
        def _(n=n):
            pl.semaphore_signal(ready.at[zz], inc=1, device_id=at_z(n), device_id_type=MESH)

        @pl.when(n < yy)
        def _(n=n):
            pl.semaphore_signal(ready.at[LINE + yy], inc=1, device_id=at_y(n), device_id_type=MESH)

    raws = (raw0, raw1, raw2, raw3)
    rows_own = pl.ds(pl.multiple_of(HALO + core * OWN, 16), OWN)
    rows_other = pl.ds(pl.multiple_of(HALO + other * OWN, 16), OWN)
    own_copy.wait()
    for b in range(4):
        w_copies[b].wait()
        raws[b][rows_own, :] = dot(hid[0:OWN, :], wbuf[b]).astype(BF16).astype(F32)
    for cp in w_copies[4:]:
        cp.start()
    st_copy.start()
    wo_copy.start()
    for cp in swaps:
        cp.wait_recv()

    @pl.when(chip > 0)
    def _():
        halo0.wait_recv()

    @pl.when(chip == 0)
    def _():
        hid[ROWS : ROWS + HALO, :] = jnp.zeros((HALO, DM), BF16)

    taps_of = (
        lambda: conv_query[:, col256].astype(F32),
        lambda: conv_key[:, col256].astype(F32),
        lambda: conv_value[:, pl.ds(pl.multiple_of(core * 512, 256), 256)].astype(F32),
        lambda: conv_value[:, pl.ds(pl.multiple_of(core * 512 + 256, 256), 256)].astype(F32),
    )
    for b in range(4):
        raw = raws[b]
        rest = dot(hid[OWN : ROWS + HALO, :], wbuf[b]).astype(BF16).astype(F32)
        raw[rows_other, :] = rest[:OWN]
        raw[0:HALO, :] = rest[OWN:]
        taps = taps_of[b]()
        for t in range(NC):
            pre = jnp.zeros((CH, 256), F32)
            for i in range(4):
                pre = pre + taps[i : i + 1, :] * raw[pl.ds(HALO - 3 + i + t * CH, CH), :]
            act = silu(pre)
            r = pl.ds(t * CH, CH)
            if b < 2:
                for g in range(2):
                    a = act[:, g * 128 : (g + 1) * 128]
                    n = a * lax.rsqrt(jnp.sum(a * a, axis=-1, keepdims=True) + 1e-6)
                    if b == 0:
                        qs[r, g * 128 : (g + 1) * 128] = (n * 128 ** (-0.5)).astype(BF16)
                    else:
                        ks[r, g * 128 : (g + 1) * 128] = n.astype(BF16)
            else:
                vs[r, (b - 2) * 256 : (b - 1) * 256] = act

    head_row = lax.broadcasted_iota(jnp.int32, (HEADS, 1), 0)

    def column_of(ref):
        v = jnp.zeros((HEADS, 1), F32)
        for h in range(HEADS):
            v = jnp.where(head_row == h, ref[core * HEADS + h], v)
        return v

    rate = -jnp.exp(column_of(decay_log))
    ti = lax.broadcasted_iota(jnp.int32, (CH, CH), 0)
    tj = lax.broadcasted_iota(jnp.int32, (CH, CH), 1)
    incl = ti >= tj
    ones_up = jnp.where(ti <= tj, 1.0, 0.0).astype(F32)
    w_gates = jnp.concatenate([w_decay[...].astype(F32), w_beta[...].astype(F32)], 0).astype(BF16)
    lg = dot_nt(w_gates, hid[0:ROWS, :])
    logits = jnp.concatenate(
        [jnp.where(core == 0, lg[:, :OWN], lg[:, OWN:]), jnp.where(core == 0, lg[:, OWN:], lg[:, :OWN])], 1
    )
    u = jnp.where(core == 0, logits[0:4], logits[4:8]) + column_of(decay_bias)
    glog = rate * (jnp.maximum(u, 0.0) + jnp.log1p(jnp.exp(-jnp.abs(u))))
    strength = jax.nn.sigmoid(jnp.where(core == 0, logits[8:12], logits[12:16]) + column_of(beta_bias))
    pad4 = jnp.zeros((4, CH), F32)
    for t in range(NC):
        cols = slice(t * CH, (t + 1) * CH)
        g8 = jnp.concatenate([glog[:, cols], pad4], 0)
        cr8 = jnp.dot(g8, ones_up, precision=lax.Precision.HIGHEST, preferred_element_type=F32)
        cumt[t] = cr8
        stacked = jnp.concatenate([cr8, strength[:, cols], jnp.zeros((CH - 12, CH), F32)], 0)
        cum[t] = stacked.T

    z128 = jnp.zeros((CH, CH), BF16)

    def pair_diag(m):
        return jnp.concatenate(
            [jnp.concatenate([m[:, :128], z128], 1), jnp.concatenate([z128, m[:, 128:]], 1)], 0
        )

    pi = lax.broadcasted_iota(jnp.int32, (CH, 256), 0)
    pj = lax.broadcasted_iota(jnp.int32, (CH, 256), 1) % 128
    pxor = pi ^ pj
    row16 = lax.broadcasted_iota(jnp.int32, (16, 128), 0)

    def systems(c, g):
        r = chunk_rows(c)
        cc_all = cum[c]
        cr_all = cumt[c]
        k = ks[r, g * 128 : (g + 1) * 128]
        q = qs[r, g * 128 : (g + 1) * 128]
        both = dot_nt(jnp.concatenate([k, q], 0), k)
        kk, qk = both[:CH], both[CH:]
        for e in range(2):
            h = 2 * g + e
            diff = cc_all[:, h : h + 1] - cr_all[h : h + 1, :]
            ratio = jnp.exp(jnp.where(incl, diff, -1e30))
            lo = jnp.where(ti > tj, cc_all[:, 8 + h : 9 + h] * ratio * kk, 0.0)
            low[c * 2 + g, :, e * 128 : (e + 1) * 128] = lo.astype(BF16)
            att[c * 4 + h] = (ratio * qk).astype(BF16)
            tri[c * 2 + g, :, e * 128 : (e + 1) * 128] = jnp.where(
                ti == tj, 1.0, jnp.where((ti ^ tj) == 1, -lo, 0.0)
            ).astype(BF16)

    def invert():
        pairs = range(2 * NC)

        def double(level, size):
            mask = (pxor >= size) & (pxor < 2 * size)
            prods = []
            for p in pairs:
                lm = jnp.where(mask, low[p].astype(F32), 0.0).astype(BF16)
                prods.append(dot(tri[p], pair_diag(lm)).astype(BF16))
            for p, prod in zip(pairs, prods):
                t_old = tri[p]
                y = dot(prod, pair_diag(t_old))
                tri[p] = (t_old.astype(F32) - y).astype(BF16)
            return size * 2

        for level in range(6):
            double(level, 2 << level)

    def unit(c, g):
        r = chunk_rows(c)
        cc_all = cum[c]
        cr_all = cumt[c]
        k = ks[r, g * 128 : (g + 1) * 128].astype(F32)
        kt = k.T
        for e in range(2):
            h = 2 * g + e
            be = cc_all[:, 8 + h : 9 + h]
            cc = cc_all[:, h : h + 1]
            cr = cr_all[h : h + 1, :]
            tail_w = jnp.exp(cr[:, 127:128] - cr)
            rhs = jnp.concatenate([be * vs[r, h * 128 : (h + 1) * 128], (be * jnp.exp(cc)) * k], 1)
            u = dot(tri[c * 2 + g, :, e * 128 : (e + 1) * 128], rhs.astype(BF16)).astype(BF16)
            uw[c * 4 + h] = u
            ee[c * 4 + h] = dot((kt * tail_w).astype(BF16), u)

    def map_of(heads):
        s_cur, b_cur, a_cur = {}, {}, {}
        for h in heads:
            e0 = ee[h]
            s_cur[h] = e0[:, :128]
            b_cur[h] = -e0[:, 128:]
            a_cur[h] = jnp.exp(cumt[0, h : h + 1, 127:128])
            sb[h] = jnp.zeros((128, 256), BF16)
            ab[0, h : h + 1, :] = jnp.ones((1, 128), F32)
        for c in range(1, NC):
            for h in heads:
                s, bm, a = s_cur[h], b_cur[h], a_cur[h]
                packed = jnp.concatenate([s, bm], 1).astype(BF16)
                sb[c * 4 + h] = packed
                ab[c, h : h + 1, :] = jnp.broadcast_to(a, (1, 128))
                e_c = ee[c * 4 + h]
                m_c = e_c[:, 128:]
                p = dot(m_c.astype(BF16), packed)
                al = jnp.exp(cumt[c, h : h + 1, 127:128])
                s_cur[h] = al * s - p[:, :128] + e_c[:, :128]
                b_cur[h] = al * bm - a * m_c - p[:, 128:]
                a_cur[h] = a * al
        for h in heads:
            a_full = jnp.broadcast_to(a_cur[h], (16, 128))
            a_hi = a_full.astype(BF16).astype(F32)
            send[h, 0:128, :] = b_cur[h].T.astype(BF16)
            send[h, 128:256, :] = s_cur[h].T.astype(BF16)
            send[h, 256:272, :] = jnp.where(row16 < 8, a_hi, a_full - a_hi).astype(BF16)

    def to_line(z):
        return remote(send.at[z], recv.at[zz], msend.at[z], mrecv.at[zz], at_z(z))

    def total_to(y):
        return remote(tsend, trecv.at[yy], tsems.at[y], tsems.at[LINE + yy], at_y(y))

    half = pl.ds(128, 128)

    def state_to(y):
        return remote(tsend.at[half], trecv.at[0, half], tsems.at[y], tsems.at[LINE], at_y(y))

    def give(z):
        return remote(step_out.at[z], entering.at[zz], osend.at[z], orecv.at[zz], at_z(z))

    for c in range(NC):
        for g in range(2):
            systems(c, g)
    invert()
    for c in range(NC):
        for g in range(2):
            unit(c, g)
    map_of(range(HEADS))

    for z in range(1, LINE):
        @pl.when(z > zz)
        def _(z=z):
            pl.semaphore_wait(ready.at[z], 1)

    @pl.when(chip < LAST)
    def _():
        for k in (2, 3, 1):
            to_line(lax.rem(zz + k, LINE)).start()

    recv[zz] = send[zz]

    def local_part(c, carry):
        r = chunk_rows(c)
        cc_all = cum[c]
        a_all = ab[c]
        for h in range(HEADS):
            g = h // 2
            q = qs[r, g * 128 : (g + 1) * 128].astype(F32)
            o = dot(att[c * 4 + h], uw[c * 4 + h])
            qeff = jnp.exp(cc_all[:, h : h + 1]) * q - o[:, 128:]
            rr = dot(qeff.astype(BF16), sb[c * 4 + h])
            outloc[r, h * 128 : (h + 1) * 128] = o[:, :128] + rr[:, :128]
            reach[r, h * 128 : (h + 1) * 128] = (a_all[h : h + 1, :] * qeff + rr[:, 128:]).astype(BF16)
        return carry

    run(local_part)

    def arrived(z):
        @pl.when(z != zz)
        def _():
            remote(send.at[0], recv.at[z], msend.at[0], mrecv.at[z], partner).wait_recv()

    def factor(rows):
        v = rows.astype(F32)
        return v[0:1, :] + v[8:9, :]

    def split(a):
        full = jnp.broadcast_to(a, (16, 128))
        hi = full.astype(BF16).astype(F32)
        return jnp.where(row16 < 8, hi, full - hi).astype(BF16)

    def follow(x, a, m):
        bt = recv[m, 0:128, :]
        a_m = factor(recv[m, 256:272, :])
        after = jnp.concatenate([a * bt.astype(F32), recv[m, 128:256, :].astype(F32)], 0)
        return a_m * x + dot(x.astype(BF16), bt) + after, a * a_m

    st_copy.wait()
    st0[...] = st0[...].T
    for z in range(LINE - 1):
        arrived(z)
    x = recv[0, 0:256, :].astype(F32)
    a = factor(recv[0, 256:272, :])
    for z in range(1, LINE):
        pre_x[z - 1] = x
        pre_a[z - 1, 0:1, :] = a
        if z < LINE - 1:
            x, a = follow(x, a, z)

    @pl.when(yy < LINE - 1)
    def _():
        arrived(LINE - 1)
        t, t_a = follow(pre_x[LINE - 2], pre_a[LINE - 2, 0:1, :], LINE - 1)
        for y in range(1, LINE):
            @pl.when(y > yy)
            def _(y=y):
                pl.semaphore_wait(ready.at[LINE + y], 1)

        @pl.when(yy == 0)
        def _():
            s = st0[...]
            tsend[128:256, :] = (t_a * s + dot(s.astype(BF16), t[0:128].astype(BF16)) + t[128:256]).astype(BF16)
            for y in range(1, LINE):
                state_to(y).start()

        @pl.when(yy > 0)
        def _():
            tsend[0:256, :] = t.astype(BF16)
            tsend[256:272, :] = split(t_a)
            for y in range(2, LINE):
                @pl.when(y > yy)
                def _(y=y):
                    total_to(y).start()

    for b in range(2):
        w_copies[4 + b].wait()
    gain = jnp.concatenate([norm_gain[...].reshape(1, 128)] * 2, 1)

    def gate_rows(t, carry):
        r = chunk_rows(t)
        h_rows = hid[chunk_rows(t), :]
        for b in range(2):
            zs[r, b * 256 : (b + 1) * 256] = silu(dot(h_rows, wbuf[4 + b])) * gain
        return carry

    run(gate_rows)

    @pl.when(yy > 0)
    def _():
        remote(tsend.at[half], trecv.at[0, half], tsems.at[0], tsems.at[LINE], partner).wait_recv()
        st0[...] = trecv[0, 128:256, :].astype(F32)

    for y in range(1, LINE - 1):
        @pl.when(y < yy)
        def _(y=y):
            remote(tsend, trecv.at[y], tsems.at[0], tsems.at[LINE + y], partner).wait_recv()
            s = st0[...]
            st0[...] = (
                factor(trecv[y, 256:272, :]) * s
                + dot(s.astype(BF16), trecv[y, 0:128, :])
                + trecv[y, 128:256, :].astype(F32)
            )

    s_line = st0[...]
    s_bf = s_line.astype(BF16)
    step_out[0] = s_bf
    for z in range(1, LINE):
        step_out[z] = (
            pre_a[z - 1, 0:1, :] * s_line + dot(s_bf, pre_x[z - 1, 0:128, :].astype(BF16)) + pre_x[z - 1, 128:256, :]
        ).astype(BF16)
    for k in (2, 3, 1):
        give(lax.rem(zz + k, LINE)).start()
    entering[zz] = step_out[zz]
    for z in range(LINE):
        @pl.when(z != zz)
        def _(z=z):
            remote(step_out.at[0], entering.at[z], osend.at[0], orecv.at[z], partner).wait_recv()

    def finish(side, x, put):
        r = pl.ds(pl.multiple_of(side * OWN + x * 64, 64), 64)
        rz = pl.ds(pl.multiple_of(lax.select(side == core, 0, OWN) + x * 64, 64), 64)
        for h in range(HEADS):
            cols = slice(h * 128, (h + 1) * 128)
            o = outloc[r, cols] + dot_nt(reach[r, cols], entering[h])
            n = o * lax.rsqrt(jnp.mean(o * o, axis=-1, keepdims=True) + 1e-6) * zs[rz, cols]
            put(cols, n.astype(BF16))

    def to_partner(i, x):
        def put(cols, v):
            nsend[i, :, cols] = v

        finish(other, x, put)

    def keep(i, x):
        def put(cols, v):
            nfull[core, i, :, cols] = v

        finish(core, x, put)

    def block(i, n0, width):
        cols = slice(n0, n0 + width)
        return dot(nfull[0, i], wo[0:512, cols]) + dot(nfull[1, i], wo[512:1024, cols])

    def fill(dst, i, n0):
        for j in range(2):
            dst[:, j * 512 : (j + 1) * 512] = block(i, n0 + j * 512, 512).astype(BF16)

    n_first = remote(nsend.at[0], nfull.at[core, 0], nsem.at[0], nsem.at[2], partner)
    n_rest = remote(nsend.at[pl.ds(1, 3)], nfull.at[core, pl.ds(1, 3)], nsem.at[1], nsem.at[3], partner)
    to_partner(0, across)
    n_first.start()
    keep(0, across)
    to_partner(1, right)
    wo_copy.wait()
    n_first.wait_recv()

    relay_r = remote(rs_send.at[0], rs_relay.at[0], rsend.at[0], rrecv.at[0], at_x(right))
    relay_l = remote(rs_send.at[1], rs_relay.at[1], rsend.at[1], rrecv.at[1], at_x(left))
    direct_r = remote(rs_send.at[2], rs_arr.at[0], rsend.at[2], rrecv.at[2], at_x(right))
    direct_l = remote(rs_send.at[3], rs_arr.at[1], rsend.at[3], rrecv.at[3], at_x(left))
    sum_r = remote(rs_send.at[4], rs_arr.at[2], rsend.at[4], rrecv.at[4], at_x(right))
    sum_l = remote(rs_send.at[5], rs_arr.at[3], rsend.at[5], rrecv.at[5], at_x(left))
    fill(rs_send.at[0], 0, 0)
    relay_r.start()
    fill(rs_send.at[1], 0, 1024)
    relay_l.start()
    to_partner(2, left)
    to_partner(3, xx)
    n_rest.start()
    for i, x in ((1, right), (2, left), (3, xx)):
        keep(i, x)
    n_rest.wait_recv()
    fill(rs_send.at[2], 1, 1024)
    direct_r.start()
    fill(rs_send.at[3], 2, 0)
    direct_l.start()
    for j in range(2):
        rs_hold[0, :, j * 512 : (j + 1) * 512] = block(1, j * 512, 512)
    for j in range(2):
        rs_hold[1, :, j * 512 : (j + 1) * 512] = block(2, 1024 + j * 512, 512)
    relay_r.wait_recv()
    rs_send[4] = (rs_hold[0] + rs_relay[0].astype(F32)).astype(BF16)
    sum_r.start()
    relay_l.wait_recv()
    rs_send[5] = (rs_hold[1] + rs_relay[1].astype(F32)).astype(BF16)
    sum_l.start()
    for j in range(4):
        rs_own[:, j * 512 : (j + 1) * 512] = block(3, j * 512, 512)
    direct_r.wait_recv()
    direct_l.wait_recv()
    rs_own[:, 0:1024] += rs_arr[1].astype(F32)
    rs_own[:, 1024:2048] += rs_arr[0].astype(F32)
    sum_r.wait_recv()
    out[:, 0:1024] = (rs_own[:, 0:1024] + rs_arr[2].astype(F32)).astype(BF16)
    sum_l.wait_recv()
    out[:, 1024:2048] = (rs_own[:, 1024:2048] + rs_arr[3].astype(F32)).astype(BF16)

    for cp in swaps:
        cp.wait_send()

    @pl.when(sends_halo)
    def _():
        halo0.wait_send()
        halo1.wait_send()

    for n in range(LINE):
        @pl.when((n != zz) & (chip < LAST))
        def _(n=n):
            to_line(n).wait_send()

        @pl.when((n > yy) & (yy > 0))
        def _(n=n):
            total_to(n).wait_send()

        if n > 0:
            @pl.when(yy == 0)
            def _(n=n):
                state_to(n).wait_send()

        @pl.when(n != zz)
        def _(n=n):
            give(n).wait_send()

    n_first.wait_send()
    n_rest.wait_send()
    for cp in (relay_r, relay_l, direct_r, direct_l, sum_r, sum_l):
        cp.wait_send()


def on_device(*args):
    any_space = pl.BlockSpec(memory_space=pl.ANY)
    vmem = pl.BlockSpec(memory_space=pltpu.VMEM)
    smem = pl.BlockSpec(memory_space=pltpu.SMEM)
    dma = pltpu.SemaphoreType.DMA
    return pl.pallas_call(
        kernel,
        out_shape=jax.ShapeDtypeStruct((64, DM), BF16),
        in_specs=[any_space] * 5 + [vmem] * 5 + [smem] * 3 + [vmem] + [any_space] * 2,
        out_specs=vmem,
        scratch_shapes=[
            pltpu.VMEM((HALO + ROWS, DM), BF16),
            pltpu.VMEM((6, DM, 256), BF16),
            pltpu.VMEM((1024, DM), BF16),
            pltpu.VMEM((128, 128), F32),
            *[pltpu.VMEM((HALO + ROWS, 256), F32)] * 4,
            pltpu.VMEM((ROWS, 256), BF16),
            pltpu.VMEM((ROWS, 256), BF16),
            pltpu.VMEM((ROWS, 512), F32),
            pltpu.VMEM((ROWS, 512), F32),
            pltpu.VMEM((NC, CH, 128), F32),
            pltpu.VMEM((NC, 8, CH), F32),
            pltpu.VMEM((8, CH, 256), BF16),
            pltpu.VMEM((8, CH, 256), BF16),
            pltpu.VMEM((16, CH, CH), BF16),
            pltpu.VMEM((16, CH, 256), BF16),
            pltpu.VMEM((16, 128, 256), F32),
            pltpu.VMEM((16, 128, 256), BF16),
            pltpu.VMEM((NC, 8, 128), F32),
            pltpu.VMEM((ROWS, 512), BF16),
            pltpu.VMEM((ROWS, 512), F32),
            pltpu.VMEM((HEADS, MSG, 128), BF16),
            pltpu.VMEM((LINE, MSG, 128), BF16),
            pltpu.VMEM((MSG, 128), BF16),
            pltpu.VMEM((LINE, MSG, 128), BF16),
            pltpu.VMEM((LINE - 1, 256, 128), F32),
            pltpu.VMEM((LINE - 1, 8, 128), F32),
            pltpu.VMEM((LINE, 128, 128), BF16),
            pltpu.VMEM((HEADS, 128, 128), BF16),
            pltpu.VMEM((4, 64, 512), BF16),
            pltpu.VMEM((2, 4, 64, 512), BF16),
            pltpu.VMEM((6, 64, 1024), BF16),
            pltpu.VMEM((2, 64, 1024), BF16),
            pltpu.VMEM((4, 64, 1024), BF16),
            pltpu.VMEM((64, DM), F32),
            pltpu.VMEM((2, 64, 1024), F32),
            dma((5,)),
            dma((6,)),
            dma((8,)),
            dma((3,)),
            dma((HEADS,)),
            dma((LINE,)),
            dma((2 * LINE,)),
            dma((LINE,)),
            dma((LINE,)),
            dma((4,)),
            dma((6,)),
            dma((6,)),
            pltpu.SemaphoreType.REGULAR((2 * LINE,)),
        ],
        compiler_params=pltpu.CompilerParams(
            collective_id=0, has_side_effects=True, vmem_limit_bytes=56 * 1024 * 1024
        ),
    )(*args[:5], args[5].T, args[6].T, *args[7:])


def solution(mesh):
    placed = (
        P("seq", None),
        P(None, "head"),
        P(None, "head"),
        P(None, "head"),
        P(None, "head"),
        P(None, "head"),
        P(None, "head"),
        P(None, "head"),
        P(None, "head"),
        P(None, "head"),
        P("head"),
        P("head"),
        P("head"),
        P(),
        P("head", None),
        P("head", None, None),
    )
    return jax.shard_map(
        on_device, mesh=mesh, in_specs=placed, out_specs=P(("seq", "head"), None), check_vma=False
    )
```

```python
import jax
import jax.numpy as jnp
from jax import lax
from jax.experimental import pallas as pl
from jax.experimental.pallas import tpu as pltpu
from jax.sharding import PartitionSpec as P

MESH = pl.DeviceIdType.MESH
F32 = jnp.float32
BF16 = jnp.bfloat16
HALO = 16
OWN = 256
ROWS = 512
DM = 2048
CH = 128
NC = ROWS // CH
HEADS = 4
CHIPS = 16
MSG = 272
LAST = CHIPS - 1
LINE = 4


def dot(a, b):
    return jnp.dot(a, b, preferred_element_type=F32)


def dot_nt(a, b):
    return lax.dot_general(a, b, (((1,), (1,)), ((), ())), preferred_element_type=F32)


def silu(u):
    return u * jax.nn.sigmoid(u)


def kernel(
    hidden, w_query, w_key, w_value, w_gate_z, w_decay, w_beta, conv_query, conv_key, conv_value,
    decay_log, decay_bias, beta_bias, norm_gain, w_out, state_in,
    out,
    hid, wbuf, wo, st0, raw0, raw1, raw2, raw3, qs, ks, vs, zs, cum, cumt, low, tri, att, uw, ee, sb, ab,
    reach, outloc, send, recv, tsend, trecv, pre_x, pre_a, step_out, entering, nsend, nfull, rs_send, rs_relay, rs_arr, rs_own, rs_hold,
    lsem, wsem, xsem, hsem, msend, mrecv, tsems, osend, orecv, nsem, rsend, rrecv, ready,
):
    seq = lax.axis_index("seq")
    xx = lax.axis_index("head")
    chip = seq // 2
    core = seq % 2
    other = 1 - core
    partner = (chip * 2 + other, xx)
    nxt = lax.rem(chip + 1, CHIPS)
    prv = lax.rem(chip + CHIPS - 1, CHIPS)
    right = lax.rem(xx + 1, 4)
    left = lax.rem(xx + 3, 4)
    across = lax.rem(xx + 2, 4)

    def at_x(x):
        return (seq, x)

    def local(src, dst, sem):
        return pltpu.make_async_copy(src, dst, sem)

    def remote(src, dst, s_sem, r_sem, device):
        return pltpu.make_async_remote_copy(
            src_ref=src, dst_ref=dst, send_sem=s_sem, recv_sem=r_sem, device_id=device, device_id_type=MESH
        )

    col256 = pl.ds(pl.multiple_of(core * 256, 256), 256)
    zz = lax.rem(chip, LINE)
    yy = chip // LINE

    def at_z(z):
        return ((yy * LINE + z) * 2 + core, xx)

    def at_y(y):
        return ((y * LINE + zz) * 2 + core, xx)

    def chunk_rows(c):
        return pl.ds(c * CH, CH)

    def run(step):
        for c in range(NC):
            step(c, 0)

    own_copy = local(hidden, hid.at[pl.ds(0, OWN), :], lsem.at[0])
    own_copy.start()
    w_copies = [
        local(w_query.at[:, col256], wbuf.at[0], wsem.at[0]),
        local(w_key.at[:, col256], wbuf.at[1], wsem.at[1]),
    ]
    for i in range(2):
        cols = pl.ds(pl.multiple_of(core * 512 + i * 256, 256), 256)
        w_copies.append(local(w_value.at[:, cols], wbuf.at[2 + i], wsem.at[2 + i]))
    for i in range(2):
        cols = pl.ds(pl.multiple_of(core * 512 + i * 256, 256), 256)
        w_copies.append(local(w_gate_z.at[:, cols], wbuf.at[4 + i], wsem.at[4 + i]))
    for cp in w_copies[:4]:
        cp.start()
    st_copy = local(state_in.at[core * HEADS + zz], st0, lsem.at[3])
    wo_copy = local(w_out, wo, lsem.at[4])

    barrier = pltpu.get_barrier_semaphore()

    def greet(device):
        pl.semaphore_signal(barrier, inc=1, device_id=device, device_id_type=MESH)

    greet(partner)
    greet(at_x(right))
    greet(at_x(left))

    @pl.when(chip > 0)
    def _():
        greet((prv * 2 + 1, xx))

    for n in range(1, LINE):
        @pl.when(n > zz)
        def _(n=n):
            greet(at_z(n))

        @pl.when(n > yy)
        def _(n=n):
            greet(at_y(n))

    sends_halo = (core == 1) & (chip < LAST)
    pl.semaphore_wait(barrier, 3 + zz + yy + lax.select(sends_halo, 2, 0))

    swaps = [
        remote(
            hidden.at[pl.ds(i * 64, 64), :], hid.at[pl.ds(OWN + i * 64, 64), :], xsem.at[i], xsem.at[4 + i], partner
        )
        for i in range(4)
    ]
    for cp in swaps:
        cp.start()
    tail = hidden.at[pl.ds(OWN - HALO, HALO), :]
    halo_at = hid.at[pl.ds(ROWS, HALO), :]
    halo0 = remote(tail, halo_at, hsem.at[0], hsem.at[2], (nxt * 2, xx))
    halo1 = remote(tail, halo_at, hsem.at[1], hsem.at[2], (nxt * 2 + 1, xx))

    @pl.when(sends_halo)
    def _():
        halo0.start()
        halo1.start()

    for n in range(LINE - 1):
        @pl.when(n < zz)
        def _(n=n):
            pl.semaphore_signal(ready.at[zz], inc=1, device_id=at_z(n), device_id_type=MESH)

        @pl.when(n < yy)
        def _(n=n):
            pl.semaphore_signal(ready.at[LINE + yy], inc=1, device_id=at_y(n), device_id_type=MESH)

    raws = (raw0, raw1, raw2, raw3)
    rows_own = pl.ds(pl.multiple_of(HALO + core * OWN, 16), OWN)
    rows_other = pl.ds(pl.multiple_of(HALO + other * OWN, 16), OWN)
    own_copy.wait()
    for b in range(4):
        w_copies[b].wait()
        raws[b][rows_own, :] = dot(hid[0:OWN, :], wbuf[b]).astype(BF16).astype(F32)
    for cp in w_copies[4:]:
        cp.start()
    st_copy.start()
    wo_copy.start()
    for cp in swaps[:2]:
        cp.wait_recv()
    first_half = pl.ds(pl.multiple_of(HALO + other * OWN, 16), 128)
    second_half = pl.ds(pl.multiple_of(HALO + other * OWN + 128, 16), 128)
    for b in range(4):
        raws[b][first_half, :] = dot(hid[OWN : OWN + 128, :], wbuf[b]).astype(BF16).astype(F32)
    for cp in swaps[2:]:
        cp.wait_recv()

    @pl.when(chip > 0)
    def _():
        halo0.wait_recv()

    @pl.when(chip == 0)
    def _():
        hid[ROWS : ROWS + HALO, :] = jnp.zeros((HALO, DM), BF16)

    taps_of = (
        lambda: conv_query[:, col256].astype(F32),
        lambda: conv_key[:, col256].astype(F32),
        lambda: conv_value[:, pl.ds(pl.multiple_of(core * 512, 256), 256)].astype(F32),
        lambda: conv_value[:, pl.ds(pl.multiple_of(core * 512 + 256, 256), 256)].astype(F32),
    )
    for b in range(4):
        raw = raws[b]
        rest = dot(hid[OWN + 128 : ROWS + HALO, :], wbuf[b]).astype(BF16).astype(F32)
        raw[second_half, :] = rest[:128]
        raw[0:HALO, :] = rest[128:]
        taps = taps_of[b]()
        for t in range(NC):
            pre = jnp.zeros((CH, 256), F32)
            for i in range(4):
                pre = pre + taps[i : i + 1, :] * raw[pl.ds(HALO - 3 + i + t * CH, CH), :]
            act = silu(pre)
            r = pl.ds(t * CH, CH)
            if b < 2:
                for g in range(2):
                    a = act[:, g * 128 : (g + 1) * 128]
                    n = a * lax.rsqrt(jnp.sum(a * a, axis=-1, keepdims=True) + 1e-6)
                    if b == 0:
                        qs[r, g * 128 : (g + 1) * 128] = (n * 128 ** (-0.5)).astype(BF16)
                    else:
                        ks[r, g * 128 : (g + 1) * 128] = n.astype(BF16)
            else:
                vs[r, (b - 2) * 256 : (b - 1) * 256] = act

    head_row = lax.broadcasted_iota(jnp.int32, (HEADS, 1), 0)

    def column_of(ref):
        v = jnp.zeros((HEADS, 1), F32)
        for h in range(HEADS):
            v = jnp.where(head_row == h, ref[core * HEADS + h], v)
        return v

    rate = -jnp.exp(column_of(decay_log))
    ti = lax.broadcasted_iota(jnp.int32, (CH, CH), 0)
    tj = lax.broadcasted_iota(jnp.int32, (CH, CH), 1)
    incl = ti >= tj
    ones_up = jnp.where(ti <= tj, 1.0, 0.0).astype(F32)
    w_gates = jnp.concatenate([w_decay[...].astype(F32), w_beta[...].astype(F32)], 0).astype(BF16)
    lg = dot_nt(w_gates, hid[0:ROWS, :])
    logits = jnp.concatenate(
        [jnp.where(core == 0, lg[:, :OWN], lg[:, OWN:]), jnp.where(core == 0, lg[:, OWN:], lg[:, :OWN])], 1
    )
    u = jnp.where(core == 0, logits[0:4], logits[4:8]) + column_of(decay_bias)
    glog = rate * (jnp.maximum(u, 0.0) + jnp.log1p(jnp.exp(-jnp.abs(u))))
    strength = jax.nn.sigmoid(jnp.where(core == 0, logits[8:12], logits[12:16]) + column_of(beta_bias))
    pad4 = jnp.zeros((4, CH), F32)
    for t in range(NC):
        cols = slice(t * CH, (t + 1) * CH)
        g8 = jnp.concatenate([glog[:, cols], pad4], 0)
        cr8 = jnp.dot(g8, ones_up, precision=lax.Precision.HIGHEST, preferred_element_type=F32)
        cumt[t] = cr8
        stacked = jnp.concatenate([cr8, strength[:, cols], jnp.zeros((CH - 12, CH), F32)], 0)
        cum[t] = stacked.T

    z128 = jnp.zeros((CH, CH), BF16)

    def pair_diag(m):
        return jnp.concatenate(
            [jnp.concatenate([m[:, :128], z128], 1), jnp.concatenate([z128, m[:, 128:]], 1)], 0
        )

    pi = lax.broadcasted_iota(jnp.int32, (CH, 256), 0)
    pj = lax.broadcasted_iota(jnp.int32, (CH, 256), 1) % 128
    pxor = pi ^ pj
    row16 = lax.broadcasted_iota(jnp.int32, (16, 128), 0)

    def systems(c, g):
        r = chunk_rows(c)
        cc_all = cum[c]
        cr_all = cumt[c]
        k = ks[r, g * 128 : (g + 1) * 128]
        q = qs[r, g * 128 : (g + 1) * 128]
        both = dot_nt(jnp.concatenate([k, q], 0), k)
        kk, qk = both[:CH], both[CH:]
        for e in range(2):
            h = 2 * g + e
            diff = cc_all[:, h : h + 1] - cr_all[h : h + 1, :]
            ratio = jnp.exp(jnp.where(incl, diff, -1e30))
            lo = jnp.where(ti > tj, cc_all[:, 8 + h : 9 + h] * ratio * kk, 0.0)
            low[c * 2 + g, :, e * 128 : (e + 1) * 128] = lo.astype(BF16)
            att[c * 4 + h] = (ratio * qk).astype(BF16)
            tri[c * 2 + g, :, e * 128 : (e + 1) * 128] = jnp.where(
                ti == tj, 1.0, jnp.where((ti ^ tj) == 1, -lo, 0.0)
            ).astype(BF16)

    def invert():
        pairs = range(2 * NC)

        def double(level, size):
            mask = jnp.where((pxor >= size) & (pxor < 2 * size), 1.0, 0.0).astype(BF16)
            prods = []
            for p in pairs:
                lm = low[p] * mask
                prods.append(dot(tri[p], pair_diag(lm)).astype(BF16))
            for p, prod in zip(pairs, prods):
                t_old = tri[p]
                tri[p] = t_old - dot(prod, pair_diag(t_old)).astype(BF16)
            return size * 2

        for level in range(6):
            double(level, 2 << level)

    def unit(c, g):
        r = chunk_rows(c)
        cc_all = cum[c]
        cr_all = cumt[c]
        k = ks[r, g * 128 : (g + 1) * 128].astype(F32)
        kt = k.T
        for e in range(2):
            h = 2 * g + e
            be = cc_all[:, 8 + h : 9 + h]
            cc = cc_all[:, h : h + 1]
            cr = cr_all[h : h + 1, :]
            tail_w = jnp.exp(cr[:, 127:128] - cr)
            rhs = jnp.concatenate([be * vs[r, h * 128 : (h + 1) * 128], (be * jnp.exp(cc)) * k], 1)
            u = dot(tri[c * 2 + g, :, e * 128 : (e + 1) * 128], rhs.astype(BF16)).astype(BF16)
            uw[c * 4 + h] = u
            ee[c * 4 + h] = dot((kt * tail_w).astype(BF16), u)

    def map_of(heads):
        s_cur, b_cur, a_cur = {}, {}, {}
        for h in heads:
            e0 = ee[h]
            s_cur[h] = e0[:, :128]
            b_cur[h] = -e0[:, 128:]
            a_cur[h] = jnp.exp(cumt[0, h : h + 1, 127:128])
            sb[h] = jnp.zeros((128, 256), BF16)
            ab[0, h : h + 1, :] = jnp.ones((1, 128), F32)
        for c in range(1, NC):
            for h in heads:
                s, bm, a = s_cur[h], b_cur[h], a_cur[h]
                packed = jnp.concatenate([s, bm], 1).astype(BF16)
                sb[c * 4 + h] = packed
                ab[c, h : h + 1, :] = jnp.broadcast_to(a, (1, 128))
                e_c = ee[c * 4 + h]
                m_c = e_c[:, 128:]
                p = dot(m_c.astype(BF16), packed)
                al = jnp.exp(cumt[c, h : h + 1, 127:128])
                s_cur[h] = al * s - p[:, :128] + e_c[:, :128]
                b_cur[h] = al * bm - a * m_c - p[:, 128:]
                a_cur[h] = a * al
        for h in heads:
            a_full = jnp.broadcast_to(a_cur[h], (16, 128))
            a_hi = a_full.astype(BF16).astype(F32)
            send[h, 0:128, :] = b_cur[h].T.astype(BF16)
            send[h, 128:256, :] = s_cur[h].T.astype(BF16)
            send[h, 256:272, :] = jnp.where(row16 < 8, a_hi, a_full - a_hi).astype(BF16)

    def to_line(z):
        return remote(send.at[z], recv.at[zz], msend.at[z], mrecv.at[zz], at_z(z))

    def total_to(y):
        return remote(tsend, trecv.at[yy], tsems.at[y], tsems.at[LINE + yy], at_y(y))

    half = pl.ds(128, 128)

    def state_to(y):
        return remote(tsend.at[half], trecv.at[0, half], tsems.at[y], tsems.at[LINE], at_y(y))

    def give(z):
        return remote(step_out.at[z], entering.at[zz], osend.at[z], orecv.at[zz], at_z(z))

    for c in range(NC):
        for g in range(2):
            systems(c, g)
    invert()
    for c in range(NC):
        for g in range(2):
            unit(c, g)
    map_of(range(HEADS))

    for z in range(1, LINE):
        @pl.when(z > zz)
        def _(z=z):
            pl.semaphore_wait(ready.at[z], 1)

    @pl.when(chip < LAST)
    def _():
        for k in (2, 3, 1):
            to_line(lax.rem(zz + k, LINE)).start()

    recv[zz] = send[zz]

    def local_part(c, carry):
        r = chunk_rows(c)
        cc_all = cum[c]
        a_all = ab[c]
        for h in range(HEADS):
            g = h // 2
            q = qs[r, g * 128 : (g + 1) * 128].astype(F32)
            o = dot(att[c * 4 + h], uw[c * 4 + h])
            qeff = jnp.exp(cc_all[:, h : h + 1]) * q - o[:, 128:]
            rr = dot(qeff.astype(BF16), sb[c * 4 + h])
            outloc[r, h * 128 : (h + 1) * 128] = o[:, :128] + rr[:, :128]
            reach[r, h * 128 : (h + 1) * 128] = (a_all[h : h + 1, :] * qeff + rr[:, 128:]).astype(BF16)
        return carry

    run(local_part)

    def arrived(z):
        @pl.when(z != zz)
        def _():
            remote(send.at[0], recv.at[z], msend.at[0], mrecv.at[z], partner).wait_recv()

    def factor(rows):
        v = rows.astype(F32)
        return v[0:1, :] + v[8:9, :]

    def split(a):
        full = jnp.broadcast_to(a, (16, 128))
        hi = full.astype(BF16).astype(F32)
        return jnp.where(row16 < 8, hi, full - hi).astype(BF16)

    def follow(x, a, m):
        bt = recv[m, 0:128, :]
        a_m = factor(recv[m, 256:272, :])
        after = jnp.concatenate([a * bt.astype(F32), recv[m, 128:256, :].astype(F32)], 0)
        return a_m * x + dot(x.astype(BF16), bt) + after, a * a_m

    st_copy.wait()
    st0[...] = st0[...].T
    for z in range(LINE - 1):
        arrived(z)
    x = recv[0, 0:256, :].astype(F32)
    a = factor(recv[0, 256:272, :])
    for z in range(1, LINE):
        pre_x[z - 1] = x
        pre_a[z - 1, 0:1, :] = a
        if z < LINE - 1:
            x, a = follow(x, a, z)

    @pl.when(yy < LINE - 1)
    def _():
        arrived(LINE - 1)
        t, t_a = follow(pre_x[LINE - 2], pre_a[LINE - 2, 0:1, :], LINE - 1)
        for y in range(1, LINE):
            @pl.when(y > yy)
            def _(y=y):
                pl.semaphore_wait(ready.at[LINE + y], 1)

        @pl.when(yy == 0)
        def _():
            s = st0[...]
            tsend[128:256, :] = (t_a * s + dot(s.astype(BF16), t[0:128].astype(BF16)) + t[128:256]).astype(BF16)
            for y in range(1, LINE):
                state_to(y).start()

        @pl.when(yy > 0)
        def _():
            tsend[0:256, :] = t.astype(BF16)
            tsend[256:272, :] = split(t_a)
            for y in range(2, LINE):
                @pl.when(y > yy)
                def _(y=y):
                    total_to(y).start()

    for b in range(2):
        w_copies[4 + b].wait()
    gain = jnp.concatenate([norm_gain[...].reshape(1, 128)] * 2, 1)

    def gate_rows(t, carry):
        r = chunk_rows(t)
        h_rows = hid[chunk_rows(t), :]
        for b in range(2):
            zs[r, b * 256 : (b + 1) * 256] = silu(dot(h_rows, wbuf[4 + b])) * gain
        return carry

    run(gate_rows)

    @pl.when(yy > 0)
    def _():
        remote(tsend.at[half], trecv.at[0, half], tsems.at[0], tsems.at[LINE], partner).wait_recv()
        st0[...] = trecv[0, 128:256, :].astype(F32)

    for y in range(1, LINE - 1):
        @pl.when(y < yy)
        def _(y=y):
            remote(tsend, trecv.at[y], tsems.at[0], tsems.at[LINE + y], partner).wait_recv()
            s = st0[...]
            st0[...] = (
                factor(trecv[y, 256:272, :]) * s
                + dot(s.astype(BF16), trecv[y, 0:128, :])
                + trecv[y, 128:256, :].astype(F32)
            )

    s_line = st0[...]
    s_bf = s_line.astype(BF16)
    step_out[0] = s_bf
    for z in range(1, LINE):
        step_out[z] = (
            pre_a[z - 1, 0:1, :] * s_line + dot(s_bf, pre_x[z - 1, 0:128, :].astype(BF16)) + pre_x[z - 1, 128:256, :]
        ).astype(BF16)
    for k in (2, 3, 1):
        give(lax.rem(zz + k, LINE)).start()
    entering[zz] = step_out[zz]
    for z in range(LINE):
        @pl.when(z != zz)
        def _(z=z):
            remote(step_out.at[0], entering.at[z], osend.at[0], orecv.at[z], partner).wait_recv()

    def finish(side, x, put):
        r = pl.ds(pl.multiple_of(side * OWN + x * 64, 64), 64)
        rz = pl.ds(pl.multiple_of(lax.select(side == core, 0, OWN) + x * 64, 64), 64)
        for h in range(HEADS):
            cols = slice(h * 128, (h + 1) * 128)
            o = outloc[r, cols] + dot_nt(reach[r, cols], entering[h])
            n = o * lax.rsqrt(jnp.mean(o * o, axis=-1, keepdims=True) + 1e-6) * zs[rz, cols]
            put(cols, n.astype(BF16))

    def to_partner(i, x):
        def put(cols, v):
            nsend[i, :, cols] = v

        finish(other, x, put)

    def keep(i, x):
        def put(cols, v):
            nfull[core, i, :, cols] = v

        finish(core, x, put)

    def block(i, n0, width):
        cols = slice(n0, n0 + width)
        return dot(nfull[0, i], wo[0:512, cols]) + dot(nfull[1, i], wo[512:1024, cols])

    def fill(dst, i, n0):
        for j in range(2):
            dst[:, j * 512 : (j + 1) * 512] = block(i, n0 + j * 512, 512).astype(BF16)

    n_first = remote(nsend.at[0], nfull.at[core, 0], nsem.at[0], nsem.at[2], partner)
    n_rest = remote(nsend.at[pl.ds(1, 3)], nfull.at[core, pl.ds(1, 3)], nsem.at[1], nsem.at[3], partner)
    to_partner(0, across)
    n_first.start()
    keep(0, across)
    to_partner(1, right)
    wo_copy.wait()
    n_first.wait_recv()

    relay_r = remote(rs_send.at[0], rs_relay.at[0], rsend.at[0], rrecv.at[0], at_x(right))
    relay_l = remote(rs_send.at[1], rs_relay.at[1], rsend.at[1], rrecv.at[1], at_x(left))
    direct_r = remote(rs_send.at[2], rs_arr.at[0], rsend.at[2], rrecv.at[2], at_x(right))
    direct_l = remote(rs_send.at[3], rs_arr.at[1], rsend.at[3], rrecv.at[3], at_x(left))
    sum_r = remote(rs_send.at[4], rs_arr.at[2], rsend.at[4], rrecv.at[4], at_x(right))
    sum_l = remote(rs_send.at[5], rs_arr.at[3], rsend.at[5], rrecv.at[5], at_x(left))
    fill(rs_send.at[0], 0, 0)
    relay_r.start()
    fill(rs_send.at[1], 0, 1024)
    relay_l.start()
    to_partner(2, left)
    to_partner(3, xx)
    n_rest.start()
    for i, x in ((1, right), (2, left), (3, xx)):
        keep(i, x)
    n_rest.wait_recv()
    fill(rs_send.at[2], 1, 1024)
    direct_r.start()
    fill(rs_send.at[3], 2, 0)
    direct_l.start()
    for j in range(2):
        rs_hold[0, :, j * 512 : (j + 1) * 512] = block(1, j * 512, 512)
    for j in range(2):
        rs_hold[1, :, j * 512 : (j + 1) * 512] = block(2, 1024 + j * 512, 512)
    relay_r.wait_recv()
    rs_send[4] = (rs_hold[0] + rs_relay[0].astype(F32)).astype(BF16)
    sum_r.start()
    relay_l.wait_recv()
    rs_send[5] = (rs_hold[1] + rs_relay[1].astype(F32)).astype(BF16)
    sum_l.start()
    for j in range(4):
        rs_own[:, j * 512 : (j + 1) * 512] = block(3, j * 512, 512)
    direct_r.wait_recv()
    direct_l.wait_recv()
    rs_own[:, 0:1024] += rs_arr[1].astype(F32)
    rs_own[:, 1024:2048] += rs_arr[0].astype(F32)
    sum_r.wait_recv()
    out[:, 0:1024] = (rs_own[:, 0:1024] + rs_arr[2].astype(F32)).astype(BF16)
    sum_l.wait_recv()
    out[:, 1024:2048] = (rs_own[:, 1024:2048] + rs_arr[3].astype(F32)).astype(BF16)

    for cp in swaps:
        cp.wait_send()

    @pl.when(sends_halo)
    def _():
        halo0.wait_send()
        halo1.wait_send()

    for n in range(LINE):
        @pl.when((n != zz) & (chip < LAST))
        def _(n=n):
            to_line(n).wait_send()

        @pl.when((n > yy) & (yy > 0))
        def _(n=n):
            total_to(n).wait_send()

        if n > 0:
            @pl.when(yy == 0)
            def _(n=n):
                state_to(n).wait_send()

        @pl.when(n != zz)
        def _(n=n):
            give(n).wait_send()

    n_first.wait_send()
    n_rest.wait_send()
    for cp in (relay_r, relay_l, direct_r, direct_l, sum_r, sum_l):
        cp.wait_send()


def on_device(*args):
    any_space = pl.BlockSpec(memory_space=pl.ANY)
    vmem = pl.BlockSpec(memory_space=pltpu.VMEM)
    smem = pl.BlockSpec(memory_space=pltpu.SMEM)
    dma = pltpu.SemaphoreType.DMA
    return pl.pallas_call(
        kernel,
        out_shape=jax.ShapeDtypeStruct((64, DM), BF16),
        in_specs=[any_space] * 5 + [vmem] * 5 + [smem] * 3 + [vmem] + [any_space] * 2,
        out_specs=vmem,
        scratch_shapes=[
            pltpu.VMEM((HALO + ROWS, DM), BF16),
            pltpu.VMEM((6, DM, 256), BF16),
            pltpu.VMEM((1024, DM), BF16),
            pltpu.VMEM((128, 128), F32),
            *[pltpu.VMEM((HALO + ROWS, 256), F32)] * 4,
            pltpu.VMEM((ROWS, 256), BF16),
            pltpu.VMEM((ROWS, 256), BF16),
            pltpu.VMEM((ROWS, 512), F32),
            pltpu.VMEM((ROWS, 512), F32),
            pltpu.VMEM((NC, CH, 128), F32),
            pltpu.VMEM((NC, 8, CH), F32),
            pltpu.VMEM((8, CH, 256), BF16),
            pltpu.VMEM((8, CH, 256), BF16),
            pltpu.VMEM((16, CH, CH), BF16),
            pltpu.VMEM((16, CH, 256), BF16),
            pltpu.VMEM((16, 128, 256), F32),
            pltpu.VMEM((16, 128, 256), BF16),
            pltpu.VMEM((NC, 8, 128), F32),
            pltpu.VMEM((ROWS, 512), BF16),
            pltpu.VMEM((ROWS, 512), F32),
            pltpu.VMEM((HEADS, MSG, 128), BF16),
            pltpu.VMEM((LINE, MSG, 128), BF16),
            pltpu.VMEM((MSG, 128), BF16),
            pltpu.VMEM((LINE, MSG, 128), BF16),
            pltpu.VMEM((LINE - 1, 256, 128), F32),
            pltpu.VMEM((LINE - 1, 8, 128), F32),
            pltpu.VMEM((LINE, 128, 128), BF16),
            pltpu.VMEM((HEADS, 128, 128), BF16),
            pltpu.VMEM((4, 64, 512), BF16),
            pltpu.VMEM((2, 4, 64, 512), BF16),
            pltpu.VMEM((6, 64, 1024), BF16),
            pltpu.VMEM((2, 64, 1024), BF16),
            pltpu.VMEM((4, 64, 1024), BF16),
            pltpu.VMEM((64, DM), F32),
            pltpu.VMEM((2, 64, 1024), F32),
            dma((5,)),
            dma((6,)),
            dma((8,)),
            dma((3,)),
            dma((HEADS,)),
            dma((LINE,)),
            dma((2 * LINE,)),
            dma((LINE,)),
            dma((LINE,)),
            dma((4,)),
            dma((6,)),
            dma((6,)),
            pltpu.SemaphoreType.REGULAR((2 * LINE,)),
        ],
        compiler_params=pltpu.CompilerParams(
            collective_id=0, has_side_effects=True, vmem_limit_bytes=56 * 1024 * 1024
        ),
    )(*args[:5], args[5].T, args[6].T, *args[7:])


def solution(mesh):
    placed = (
        P("seq", None),
        P(None, "head"),
        P(None, "head"),
        P(None, "head"),
        P(None, "head"),
        P(None, "head"),
        P(None, "head"),
        P(None, "head"),
        P(None, "head"),
        P(None, "head"),
        P("head"),
        P("head"),
        P("head"),
        P(),
        P("head", None),
        P("head", None, None),
    )
    return jax.shard_map(
        on_device, mesh=mesh, in_specs=placed, out_specs=P(("seq", "head"), None), check_vma=False
    )
```
